512 devices in a mesh: seq: 32 (over z, core), item: 16 (over y, x).
Axes of the slice: x: 4, y: 4, z: 16, core: 2. Of those that a mesh axis runs over, the one named last changes fastest.
Arguments:
- history: bfloat16 [16, 4096, 512], P('item', 'seq'), may hold values from -6 to 6
- w_in: bfloat16 [512, 1536], replicated, may hold values from -0.25 to 0.25
- w_out: bfloat16 [512, 512], replicated, may hold values from -0.25 to 0.25
- item_table: bfloat16 [65536, 512], P(('seq', 'item')), may hold values from -6 to 6
- w_item_in: bfloat16 [512, 1024], replicated, may hold values from -0.25 to 0.25
- w_item_out: bfloat16 [1024, 512], replicated, may hold values from -0.1875 to 0.1875
- req_rows: int32 [16, 32, 512, 2], P('item', 'seq'), may hold values from 0 to 127
- req_counts: int32 [16, 32, 512], P('item', 'seq'), may hold values from 1 to 2, as said below
- labels: int32 [16, 4096, 4], P('item', 'seq'), may hold values from -1 to 1023, as said below
Outputs:
- position_loss: float32 [16, 4096], P('item', 'seq')
- item_table_gradient: float32 [65536, 512], P(('seq', 'item'))
The draws below stay inside these ranges and needn't reach their ends.
Inputs may be any that keep to these rules, and one draw needn't show every extreme that they name: `req_rows`: slots at or beyond the block's count toward that owner are padding. `req_counts`: every history block uses all 2 slots toward some owner, and in every draw some owner is asked for 2 rows by every block. `labels`: A slot named is a used slot of the position's block; -1 names none; a slot may be named twice.
All inputs are finite; a program needn't handle non-finite values.
Results may differ from the reference program's by a relative error of at most 0.0085.
Values may be sent and summed in bfloat16 or wider, within the bound.
No kernel may reach another device: no remote copies, remote signals or barrier semaphores. Data moves between devices by JAX's collectives and lax.ppermute only.
A program may use at most 64 MiB of HBM per device.

```python
import jax
import jax.numpy as jnp
from jax import lax

D = 512
HEADS = 4
DQK = 64
F = 512
FF = 1024
LABELS = 4
CAP = 2
TOK_DEV = 128
ROWS_DEV = 128
LENGTH = 4096
USERS = 16
OWNERS = 512
ITEMS = 65536
N_SEQ = 32


def shared_counts(key):
    key = jax.random.fold_in(key, 101)
    key_base, key_full, key_crowd = jax.random.split(key, 3)
    counts = jax.random.randint(key_base, (USERS, N_SEQ, OWNERS), 1, CAP + 1)
    full_owner = jax.random.randint(key_full, (USERS, N_SEQ, 1), 0, OWNERS)
    crowded = jax.random.randint(key_crowd, (), 0, OWNERS)
    owner_ids = jnp.arange(OWNERS, dtype=jnp.int32)[None, None, :]
    filled = (owner_ids == full_owner) | (owner_ids == crowded)
    return jnp.where(filled, CAP, counts).astype(jnp.int32)


def draw_req_counts(key, part):
    return shared_counts(key)


def draw_labels(key, part):
    counts = shared_counts(key)
    key = jax.random.fold_in(key, 7)
    key_owner, key_slot, key_present = jax.random.split(key, 3)
    label_shape = (USERS, LENGTH, LABELS)
    owners = jax.random.randint(key_owner, label_shape, 0, OWNERS)
    blocks = (jnp.arange(LENGTH, dtype=jnp.int32) // TOK_DEV)[None, :, None]
    users = jnp.arange(USERS, dtype=jnp.int32)[:, None, None]
    limits = counts[users, blocks, owners]
    within = jax.random.randint(key_slot, label_shape, 0, CAP) % limits
    present = jax.random.randint(key_present, label_shape, 0, 20) >= 9
    return jnp.where(present, owners * CAP + within, -1).astype(jnp.int32)


def plant(entries, stream_key, smallest, largest):
    index_at = [jax.random.randint(jax.random.fold_in(stream_key, axis), (), 0, length) for axis, length in enumerate(entries.shape)]
    widest = entries.shape.index(max(entries.shape))
    next_to = index_at[:widest] + [(index_at[widest] + 1) % entries.shape[widest]] + index_at[widest + 1:]
    return entries.at[tuple(index_at)].set(smallest).at[tuple(next_to)].set(largest)


def shard_levels(rng, shape, cuts, least, largest):
    gain, own = 1.0, jax.random.fold_in(rng, 6)
    for dim, blocks in cuts:
        heights = jnp.exp(jax.random.uniform(jax.random.fold_in(own, dim), (blocks,), jnp.float32, least / len(cuts), largest / len(cuts)))
        gain = gain * jnp.repeat(heights, shape[dim] // blocks).reshape([-1 if axis == dim else 1 for axis in range(len(shape))])
    return gain


def normal_values(rng, shape, deviation, limit, cuts=(), kind=jnp.bfloat16):
    result = jax.random.normal(rng, shape, jnp.float32) * deviation
    if len(cuts) > 0:
        result = shard_levels(rng, shape, cuts, -0.22, 0.18) * result
    return jnp.clip(result, min=-limit, max=limit).astype(kind)


def setup_inputs(seed: int = 0) -> dict:
    key_list = jax.random.split(jax.random.key(seed), 10)
    return {
        "history": normal_values(key_list[0], (USERS, LENGTH, D), 1.0, 6.0, ((0, 16), (1, 32))),
        "w_in": normal_values(key_list[1], (D, 2 * D + 2 * HEADS * DQK), D ** -0.5, 0.25),
        "w_out": normal_values(key_list[2], (D, D), D ** -0.5, 0.25),
        "item_table": normal_values(key_list[3], (ITEMS, F), 1.0, 6.0, ((0, 512),)),
        "w_item_in": normal_values(key_list[4], (F, FF), F ** -0.5, 0.25),
        "w_item_out": normal_values(key_list[5], (FF, D), FF ** -0.5, 0.1875),
        "req_rows": plant(jax.random.randint(key_list[6], (USERS, N_SEQ, OWNERS, CAP), 0, ROWS_DEV), jax.random.fold_in(key_list[6], 1), 0, ROWS_DEV - 1).astype(jnp.int32),
        "req_counts": draw_req_counts(jax.random.fold_in(key_list[9], 71), 0),
        "labels": draw_labels(jax.random.fold_in(key_list[9], 71), 0),
    }


sharpness_divisor = 0.02
norm_eps = 1e-05
unit_eps = 1e-06

def silu_slope(inputs):
    sigma = jax.nn.sigmoid(inputs)
    return sigma * (1.0 + inputs * (1.0 - sigma))

def split_product(left, weight):
    contract = (((1,), (1,)), ((), ()))
    high = left.astype(jnp.bfloat16)
    low = (left - high.astype(jnp.float32)).astype(jnp.bfloat16)
    first = lax.dot_general(high, weight, contract, preferred_element_type=jnp.float32)
    return first + lax.dot_general(low, weight, contract, preferred_element_type=jnp.float32)

def item_forward(table_rows, w_item_in, w_item_out):
    hidden_in = jnp.dot(table_rows, w_item_in, preferred_element_type=jnp.float32)
    hidden = jax.nn.silu(hidden_in).astype(jnp.bfloat16)
    raw_embed = jnp.dot(hidden, w_item_out, preferred_element_type=jnp.float32)
    inv_norm = lax.rsqrt(lax.optimization_barrier(jnp.sum(raw_embed * raw_embed, axis=-1, keepdims=True)) + unit_eps)
    embedding = (raw_embed * inv_norm).astype(jnp.bfloat16)
    return (hidden_in, raw_embed, inv_norm, embedding)

def item_backward(hidden_in, raw_embed, inv_norm, vector_derivative_matrix, w_item_in, w_item_out):
    unit = raw_embed * inv_norm
    raw_grad = (vector_derivative_matrix - unit * lax.optimization_barrier(jnp.sum(unit * vector_derivative_matrix, axis=-1, keepdims=True))) * inv_norm
    hidden_grad = split_product(raw_grad, w_item_out)
    input_grad = hidden_grad * silu_slope(hidden_in)
    return split_product(input_grad, w_item_in)

def block_loss(customer_vector_entries, catalog_entries, counts, label_slots):
    slot_total = catalog_entries.shape[0]
    capacity = slot_total // counts.shape[0]
    similarity_matrix = lax.dot_general(customer_vector_entries, catalog_entries, (((1,), (1,)), ((), ())), preferred_element_type=jnp.float32) / sharpness_divisor
    used = (jnp.arange(capacity, dtype=jnp.int32)[None, :] < counts[:, None]).reshape(-1)
    exponent = jnp.where(used[None, :], jnp.exp(similarity_matrix), 0.0)
    total = lax.optimization_barrier(jnp.sum(exponent, axis=-1))
    log_total = jnp.log(total)
    slot_ids = jnp.arange(slot_total, dtype=jnp.int32)
    positive_hits = jnp.zeros(similarity_matrix.shape, jnp.float32)
    for column in range(label_slots.shape[1]):
        positive_hits = positive_hits + (label_slots[:, column][:, None] == slot_ids[None, :]).astype(jnp.float32)
    positives = lax.optimization_barrier(jnp.sum((label_slots >= 0).astype(jnp.float32), axis=-1))
    divisor = jnp.maximum(positives, 1.0)
    position_loss = lax.optimization_barrier(jnp.sum(positive_hits * (log_total[:, None] - similarity_matrix), axis=-1)) / divisor
    probability = exponent / total[:, None]
    similarity_derivative = ((positives / divisor)[:, None] * probability - positive_hits / divisor[:, None]).astype(jnp.bfloat16)
    vector_derivative_matrix = lax.dot_general(similarity_derivative, customer_vector_entries, (((0,), (0,)), ((), ())), preferred_element_type=jnp.float32) / sharpness_divisor
    return (position_loss, vector_derivative_matrix)

def user_tower(history_rows, w_in, w_out):
    projected = jnp.dot(history_rows, w_in, preferred_element_type=jnp.float32)
    activated = jax.nn.silu(projected)
    gate_units = activated[:, :D]
    value_rows = activated[:, D:2 * D].astype(jnp.bfloat16)
    query_rows = activated[:, 2 * D:2 * D + HEADS * DQK].astype(jnp.bfloat16)
    key_rows = activated[:, 2 * D + HEADS * DQK:].astype(jnp.bfloat16)
    query_heads = query_rows.astype(jnp.float32).reshape(N_SEQ, TOK_DEV, HEADS, DQK)
    key_heads = key_rows.astype(jnp.float32).reshape(LENGTH, HEADS, DQK)
    value_heads = value_rows.astype(jnp.float32).reshape(LENGTH, HEADS, D // HEADS)
    key_positions = jnp.arange(LENGTH, dtype=jnp.int32)

    def attend_block(inputs):
        partition_lookups, first = inputs
        positions = first + jnp.arange(TOK_DEV, dtype=jnp.int32)
        similarity_matrix = jnp.einsum('qhd,khd->hqk', partition_lookups, key_heads) * DQK ** (-0.5)
        allowed = key_positions[None, None, :] <= positions[None, :, None]
        weights = jnp.where(allowed, jax.nn.silu(similarity_matrix), 0.0).astype(jnp.bfloat16)
        return jnp.einsum('hqk,khd->qhd', weights.astype(jnp.float32), value_heads)
    firsts = jnp.arange(N_SEQ, dtype=jnp.int32) * TOK_DEV
    attended = lax.map(attend_block, (query_heads, firsts)).reshape(LENGTH, D)
    row_mean = lax.optimization_barrier(jnp.mean(attended, axis=-1, keepdims=True))
    centered = attended - row_mean
    variance = lax.optimization_barrier(jnp.mean(centered * centered, axis=-1, keepdims=True))
    normed = centered * lax.rsqrt(variance + norm_eps)
    mixed_rows = (normed * gate_units).astype(jnp.bfloat16)
    updated = history_rows.astype(jnp.float32) + jnp.dot(mixed_rows, w_out, preferred_element_type=jnp.float32)
    scale = lax.rsqrt(lax.optimization_barrier(jnp.sum(updated * updated, axis=-1, keepdims=True)) + unit_eps)
    return (updated * scale).astype(jnp.bfloat16)

def reference(history, w_in, w_out, item_table, w_item_in, w_item_out, req_rows, req_counts, labels):

    def tower_of(history_rows):
        return user_tower(history_rows, w_in, w_out)
    customer_vector_entries = lax.map(tower_of, history)
    table_blocks = item_table.reshape(OWNERS, ROWS_DEV, F)

    def embed_block(table_rows):
        return item_forward(table_rows, w_item_in, w_item_out)[3]
    embeddings = lax.map(embed_block, table_blocks).reshape(ITEMS, D)
    owner_base = (jnp.arange(OWNERS, dtype=jnp.int32) * ROWS_DEV)[:, None]

    def block_step(row_grad, inputs):
        block_users, block_rows, block_counts, block_labels = inputs
        item_ids = (block_rows + owner_base).reshape(-1).astype(jnp.int32)
        catalog_entries = jnp.take(embeddings, item_ids, axis=0)
        position_loss, vector_derivative_matrix = block_loss(block_users, catalog_entries, block_counts, block_labels)
        return (row_grad.at[item_ids].add(vector_derivative_matrix), position_loss)
    inputs = (customer_vector_entries.reshape(USERS * N_SEQ, TOK_DEV, D), req_rows.reshape(USERS * N_SEQ, OWNERS, CAP), req_counts.reshape(USERS * N_SEQ, OWNERS), labels.reshape(USERS * N_SEQ, TOK_DEV, LABELS))
    row_grad, penalty_values = lax.scan(block_step, jnp.zeros((ITEMS, D), jnp.float32), inputs)

    def grad_block(pieces):
        table_rows, block_grad = pieces
        hidden_in, raw_embed, inv_norm, unused = item_forward(table_rows, w_item_in, w_item_out)
        return item_backward(hidden_in, raw_embed, inv_norm, block_grad, w_item_in, w_item_out)
    item_table_gradient = lax.map(grad_block, (table_blocks, row_grad.reshape(OWNERS, ROWS_DEV, D))).reshape(ITEMS, F)
    return (penalty_values.reshape(USERS, LENGTH), item_table_gradient)
```

```python
import jax
import jax.numpy as jnp
from jax import lax
from jax.experimental import pallas as pl
from jax.experimental.pallas import tpu as pltpu
from jax.sharding import Mesh
from jax.sharding import PartitionSpec as P

HEADS = 4
DQK = 64
TOK = 128
WIDTH = 512
HIDDEN = 1024
CHIPS = 16
HALF = CHIPS * TOK
PACK_ROWS = 136
SEND_ROWS = 136
CODE_SCALE = 4096.0

inverse_sharpness = 50.0
norm_eps = 1e-05
unit_eps = 1e-06

BF = jnp.bfloat16
F32 = jnp.float32
VMEM_LIMIT = 56 * 1024 * 1024

NN = (((1,), (0,)), ((), ()))
NT = (((1,), (1,)), ((), ()))


def dot(left, right, contract=NN):
    return lax.dot_general(left, right, contract, preferred_element_type=F32)


def half_silu(half):
    return half + half * jnp.tanh(half)


def silu(inputs):
    return half_silu(0.5 * inputs)


def split_product(left, weight):
    high = left.astype(BF)
    low = (left - high.astype(F32)).astype(BF)
    return dot(high, weight, NT) + dot(low, weight, NT)


def call(kernel, out_shape, n_smem, n_vmem, scratch=()):
    space = [pl.BlockSpec(memory_space=pltpu.SMEM)] * n_smem
    space += [pl.BlockSpec(memory_space=pltpu.VMEM)] * n_vmem
    return pl.pallas_call(
        kernel,
        out_shape=out_shape,
        in_specs=space,
        out_specs=jax.tree.map(lambda _: pl.BlockSpec(memory_space=pltpu.VMEM), out_shape),
        scratch_shapes=list(scratch),
        compiler_params=pltpu.CompilerParams(vmem_limit_bytes=VMEM_LIMIT),
    )


def embed_kernel(table_ref, w_in_ref, w_out_ref, hidden_in_ref, raw_ref, embedding_ref):
    hidden_in = dot(table_ref[...], w_in_ref[...])
    hidden_in_ref[...] = hidden_in
    raw = dot(silu(hidden_in).astype(BF), w_out_ref[...])
    raw_ref[...] = raw
    inv_norm = lax.rsqrt(jnp.sum(raw * raw, axis=-1, keepdims=True) + unit_eps)
    embedding_ref[...] = (raw * inv_norm).astype(BF)


def tower_kernel(
    place_ref, history_ref, w_in_ref, w_out_ref, user_ref, key_scr, value_scr, query_scr, total_scr
):
    parity = place_ref[0]

    def project(step, carry):
        rows = history_ref[step].reshape(2 * TOK, WIDTH)
        at = pl.ds(pl.multiple_of(step * 2 * TOK, 2 * TOK), 2 * TOK)
        value_scr[at, :] = silu(dot(rows, w_in_ref[:, 512:1024])).astype(BF)
        key_scr[at, :] = silu(dot(rows, w_in_ref[:, 1280:1536])).astype(BF)
        return carry

    lax.fori_loop(0, CHIPS, project, 0)

    def own_rows(pair):
        first = history_ref[2 * pair, parity]
        second = history_ref[2 * pair + 1, parity]
        return jnp.concatenate([first, second], axis=0)

    lane = lax.broadcasted_iota(jnp.int32, (2 * TOK, 2 * DQK), 1)
    row = lax.broadcasted_iota(jnp.int32, (2 * TOK, 4 * TOK), 0)
    key_at = lax.broadcasted_iota(jnp.int32, (2 * TOK, 4 * TOK), 1)
    in_second = (row >= TOK).astype(jnp.int32)
    limit = (2 * in_second + parity) * TOK + row - in_second * TOK
    allowed = key_at <= limit

    def attend(pair, carry):
        rows = own_rows(pair)
        query = (silu(dot(rows, w_in_ref[:, 1024:1280])).astype(BF) * 0.0625).astype(BF)
        for head in range(HEADS):
            both = query[:, (head // 2) * 2 * DQK : (head // 2 + 1) * 2 * DQK]
            mine = (lane >= DQK) if head % 2 else (lane < DQK)
            query_scr[head] = jnp.where(mine, both, jnp.zeros_like(both))
        total_scr[...] = jnp.zeros_like(total_scr)

        def tile(step, masked):
            at = pl.ds(pl.multiple_of(step * 4 * TOK, 4 * TOK), 4 * TOK)
            for head in range(HEADS):
                keys = key_scr[at, (head // 2) * 2 * DQK : (head // 2 + 1) * 2 * DQK]
                weights = half_silu(dot(query_scr[head], keys, NT))
                if masked:
                    weights = jnp.where(allowed, weights, 0.0)
                values = value_scr[at, head * 128 : (head + 1) * 128]
                total_scr[:, head * 128 : (head + 1) * 128] += dot(weights.astype(BF), values)

        def full(step, inner):
            tile(step, False)
            return inner

        lax.fori_loop(0, pair, full, 0)
        tile(pair, True)

        attended = total_scr[...]
        centered = attended - jnp.mean(attended, axis=-1, keepdims=True)
        variance = jnp.mean(centered * centered, axis=-1, keepdims=True)
        normed = centered * lax.rsqrt(variance + norm_eps)
        gate_units = silu(dot(rows, w_in_ref[:, 0:512]))
        mixed_rows = (normed * gate_units).astype(BF)
        updated = rows.astype(F32) + dot(mixed_rows, w_out_ref[...])
        scale = lax.rsqrt(jnp.sum(updated * updated, axis=-1, keepdims=True) + unit_eps)
        at = pl.ds(pl.multiple_of(pair * 2 * TOK, 2 * TOK), 2 * TOK)
        user_ref[at, :] = (updated * scale).astype(BF)
        return carry

    lax.fori_loop(0, CHIPS // 2, attend, 0)


def label_places(labels_ref, block, entry, chip):
    label = labels_ref[block : block + 1, entry * TOK : (entry + 1) * TOK].astype(jnp.int32)
    local = label - chip * 64
    inside = (label >= 0) & (local >= 0) & (local < 64)
    return jnp.where(inside, (local & 1) * 32 + (local >> 1), -1)


def scores_kernel(
    place_ref, table_ref, user_ref, rows_ref, used_ref, labels_ref,
    exps_ref, hits_ref, exchange_ref, entry_scr,
):
    chip = place_ref[1]
    row_ids = lax.broadcasted_iota(jnp.int32, (32, TOK), 1).astype(F32)
    for owner in range(32):
        pick = (row_ids == rows_ref[:, owner : owner + 1]).astype(BF)
        rows = dot(pick, table_ref[owner * TOK : (owner + 1) * TOK, :])
        for slot in range(2):
            for part in range(4):
                entry_scr[part, pl.ds(slot * 32 + owner, 16, stride=64), :] = rows[
                    slot * 16 : (slot + 1) * 16, part * 128 : (part + 1) * 128
                ]
    slot_ids = lax.broadcasted_iota(jnp.int32, (64, TOK), 0)
    exchange_ref[...] = jnp.zeros_like(exchange_ref)
    for block in range(CHIPS):
        entries = jnp.concatenate(
            [entry_scr[part, block * 64 : (block + 1) * 64, :] for part in range(4)], axis=1
        ).astype(BF)
        scores = dot(entries, user_ref[block * TOK : (block + 1) * TOK, :], NT) * inverse_sharpness
        used = used_ref[:, block : block + 1] >= 0.0
        exps = jnp.where(used, jnp.exp(scores), 0.0)
        exps_ref[block] = exps
        hits = jnp.zeros((64, TOK), F32)
        for entry in range(4):
            place = label_places(labels_ref, block, entry, chip)
            hits = hits + (slot_ids == place).astype(F32)
        hits_ref[block] = hits
        total = jnp.sum(exps, axis=0, keepdims=True)
        exchange_ref[:, block : block + 1, :] = jnp.broadcast_to(total[None], (CHIPS, 1, TOK))
        exchange_ref[block, 16:17, :] = jnp.sum(hits * scores, axis=0, keepdims=True)


def gradient_kernel(
    place_ref, exps_ref, hits_ref, user_ref, exchange_ref, labels_ref, index_ref,
    send_ref, loss_ref, grad_scr,
):
    chip = place_ref[1]
    sums = jnp.sum(exchange_ref[...], axis=0)
    positives = jnp.zeros((CHIPS, TOK), F32)
    for entry in range(4):
        positives = positives + (labels_ref[:, entry * TOK : (entry + 1) * TOK] >= 0.0).astype(F32)
    divisor = jnp.maximum(positives, 1.0)
    totals = sums[0:16]
    own = lax.broadcasted_iota(jnp.int32, (CHIPS, TOK), 0) == chip
    losses = (positives * jnp.log(totals) - sums[16:17]) / divisor
    loss_ref[...] = jnp.sum(jnp.where(own, losses, 0.0), axis=0, keepdims=True)
    exp_scale = positives / (divisor * totals)
    hit_scale = 1.0 / divisor
    for block in range(CHIPS):
        score_grad = (
            exps_ref[block] * exp_scale[block : block + 1]
            - hits_ref[block] * hit_scale[block : block + 1]
        ).astype(BF)
        grads = dot(score_grad, user_ref[block * TOK : (block + 1) * TOK, :]) * inverse_sharpness
        for slot in range(2):
            for part in range(4):
                at = part * 32 + slot * 16 + block
                grad_scr[pl.ds(at, 32, stride=SEND_ROWS), :] = grads[
                    slot * 32 : (slot + 1) * 32, part * 128 : (part + 1) * 128
                ]
    zeros = jnp.zeros((32, TOK), F32)
    for extra in range(8):
        grad_scr[pl.ds(TOK + extra, 32, stride=SEND_ROWS), :] = index_ref[...] if extra == 0 else zeros
    send_ref[...] = grad_scr[...].astype(BF)


def owner_kernel(
    arrived_ref, index_ref, hidden_in_ref, raw_ref, w_in_ref, w_out_ref, gradient_ref, rows_scr
):
    row_ids = lax.broadcasted_iota(jnp.int32, (TOK, TOK), 0).astype(F32)
    row_grad = jnp.zeros((TOK, WIDTH), F32)
    for group in range(8):
        index = jnp.zeros((1, TOK), F32)
        for member in range(4):
            sender = group * 4 + member
            index = index + index_ref[sender : sender + 1, :]
            for part in range(4):
                rows_scr[member * 32 : (member + 1) * 32, part * 128 : (part + 1) * 128] = arrived_ref[
                    sender, part * 32 : (part + 1) * 32, :
                ]
        pick = (row_ids == index).astype(BF)
        row_grad = row_grad + dot(pick, rows_scr[...])
    raw = raw_ref[...]
    inv_norm = lax.rsqrt(jnp.sum(raw * raw, axis=-1, keepdims=True) + unit_eps)
    unit = raw * inv_norm
    raw_grad = (row_grad - unit * jnp.sum(unit * row_grad, axis=-1, keepdims=True)) * inv_norm
    hidden_grad = split_product(raw_grad, w_out_ref[...])
    hidden_in = hidden_in_ref[...]
    sigma = 0.5 * jnp.tanh(0.5 * hidden_in) + 0.5
    input_grad = hidden_grad * (sigma * (1.0 + hidden_in * (1.0 - sigma)))
    gradient_ref[...] = split_product(input_grad, w_in_ref[...])


def on_device(
    history, w_in, w_out, item_table, w_item_in, w_item_out, req_rows, req_counts, labels
):
    chip = lax.axis_index("z")
    core = lax.axis_index("core")
    place = jnp.stack([core, chip]).astype(jnp.int32)

    with jax.named_scope("embed"):
        hidden_in, raw_embed, embedding = call(
            embed_kernel,
            (
                jax.ShapeDtypeStruct((TOK, HIDDEN), F32),
                jax.ShapeDtypeStruct((TOK, WIDTH), F32),
                jax.ShapeDtypeStruct((TOK, WIDTH), BF),
            ),
            0,
            3,
        )(item_table, w_item_in, w_item_out)

    with jax.named_scope("pack"):
        wanted = req_rows[0, 0]
        used = jnp.arange(2, dtype=jnp.int32)[None, :] < req_counts[0, 0][:, None]
        wanted = jnp.where(used, wanted, -1)
        packed = jnp.concatenate(
            [
                (history[0].astype(F32) * CODE_SCALE).astype(jnp.float16),
                wanted.reshape(2, WIDTH).astype(jnp.float16),
                labels[0].T.reshape(1, WIDTH).astype(jnp.float16),
                jnp.zeros((PACK_ROWS - TOK - 3, WIDTH), jnp.float16),
            ],
            axis=0,
        )
        packed, embedding = lax.optimization_barrier((packed, embedding))

    with jax.named_scope("table_gather"):
        table = lax.all_gather(embedding, ("core", "item"), axis=0, tiled=True)

    with jax.named_scope("history_gather"):
        gathered = lax.all_gather(packed, ("z", "core"), axis=0, tiled=True)

    with jax.named_scope("unpack"):
        gathered = gathered.reshape(CHIPS, 2, PACK_ROWS, WIDTH)
        histories = (gathered[:, :, :TOK].astype(F32) * (1.0 / CODE_SCALE)).astype(BF)
        extras = lax.dynamic_slice(
            gathered, (0, core, TOK, 0), (CHIPS, 1, 8, WIDTH)
        ).reshape(CHIPS, 8, WIDTH).astype(F32)
        label_rows = extras[:, 2]
        asked = lax.dynamic_slice(extras[:, 0:2].reshape(CHIPS, 1024), (0, chip * 64), (CHIPS, 64))
        asked = asked.reshape(CHIPS, 32, 2)
        by_owner = asked.transpose(2, 0, 1).reshape(32, 32)
        by_block = asked.transpose(2, 1, 0).reshape(64, CHIPS)
        sender = core * 16 + lax.axis_index("item")
        quarter = (jnp.arange(4) == sender % 4).astype(F32)
        index = (by_owner.T[:, None, :] * quarter[None, :, None]).reshape(32, TOK)

    with jax.named_scope("tower"):
        user_rows = call(
            tower_kernel,
            jax.ShapeDtypeStruct((HALF, WIDTH), BF),
            1,
            3,
            [
                pltpu.VMEM((2 * HALF, HEADS * DQK), BF),
                pltpu.VMEM((2 * HALF, WIDTH), BF),
                pltpu.VMEM((HEADS, 2 * TOK, 2 * DQK), BF),
                pltpu.VMEM((2 * TOK, WIDTH), F32),
            ],
        )(place, histories, w_in, w_out)

    with jax.named_scope("scores"):
        exps, hits, exchange = call(
            scores_kernel,
            (
                jax.ShapeDtypeStruct((CHIPS, 64, TOK), F32),
                jax.ShapeDtypeStruct((CHIPS, 64, TOK), F32),
                jax.ShapeDtypeStruct((CHIPS, 24, TOK), F32),
            ),
            1,
            5,
            [pltpu.VMEM((4, 1024, 128), F32)],
        )(place, table, user_rows, by_owner, by_block, label_rows)

    with jax.named_scope("totals_exchange"):
        exchange = lax.all_to_all(exchange, "z", split_axis=0, concat_axis=0, tiled=True)

    with jax.named_scope("gradient_rows"):
        send, loss = call(
            gradient_kernel,
            (
                jax.ShapeDtypeStruct((32 * SEND_ROWS, 128), BF),
                jax.ShapeDtypeStruct((1, TOK), F32),
            ),
            1,
            6,
            [pltpu.VMEM((32 * SEND_ROWS, 128), F32)],
        )(place, exps, hits, user_rows, exchange, label_rows, index)

    with jax.named_scope("gradient_send"):
        arrived = lax.all_to_all(
            send.reshape(32, SEND_ROWS, 128), ("core", "item"), split_axis=0, concat_axis=0, tiled=True
        )

    with jax.named_scope("owner"):
        gradient = call(
            owner_kernel,
            jax.ShapeDtypeStruct((TOK, WIDTH), F32),
            0,
            6,
            [pltpu.VMEM((TOK, WIDTH), BF)],
        )(arrived, arrived[:, TOK].astype(F32), hidden_in, raw_embed, w_item_in, w_item_out)
    return (loss, gradient)


def solution(mesh):
    split = Mesh(mesh.devices.reshape(CHIPS, 2, 16), ("z", "core", "item"))
    rows = ("z", "core")
    placed = (
        P("item", rows, None),
        P(),
        P(),
        P(("z", "core", "item"), None),
        P(),
        P(),
        P("item", rows, None, None),
        P("item", rows, None),
        P("item", rows, None),
    )
    return jax.shard_map(
        on_device,
        mesh=split,
        in_specs=placed,
        out_specs=(P("item", rows), P(("z", "core", "item"), None)),
        check_vma=False,
    )
```

```python
import jax
import jax.numpy as jnp
from jax import lax
from jax.experimental import pallas as pl
from jax.experimental.pallas import tpu as pltpu
from jax.sharding import Mesh
from jax.sharding import PartitionSpec as P

HEADS = 4
DQK = 64
TOK = 128
WIDTH = 512
HIDDEN = 1024
CHIPS = 16
HALF = CHIPS * TOK
TILE = 512
PACK_ROWS = 144
SEND_ROWS = 136
RANGE = 6.0
CODES = 32760.0

inverse_sharpness = 50.0
norm_eps = 1e-05
unit_eps = 1e-06

BF = jnp.bfloat16
F32 = jnp.float32
VMEM_LIMIT = 56 * 1024 * 1024

NN = (((1,), (0,)), ((), ()))
NT = (((1,), (1,)), ((), ()))


def dot(left, right, contract=NN):
    return lax.dot_general(left, right, contract, preferred_element_type=F32)


def half_silu(half):
    return half + half * jnp.tanh(half)


def silu(inputs):
    return half_silu(0.5 * inputs)


def split_product(left, weight):
    high = left.astype(BF)
    low = (left - high.astype(F32)).astype(BF)
    return dot(high, weight, NT) + dot(low, weight, NT)


def call(kernel, out_shape, n_smem, n_vmem, scratch=()):
    space = [pl.BlockSpec(memory_space=pltpu.SMEM)] * n_smem
    space += [pl.BlockSpec(memory_space=pltpu.VMEM)] * n_vmem
    return pl.pallas_call(
        kernel,
        out_shape=out_shape,
        in_specs=space,
        out_specs=jax.tree.map(lambda _: pl.BlockSpec(memory_space=pltpu.VMEM), out_shape),
        scratch_shapes=list(scratch),
        compiler_params=pltpu.CompilerParams(vmem_limit_bytes=VMEM_LIMIT),
    )


def prepare_kernel(
    history_ref, wanted_ref, counts_ref, labels_ref, table_ref, w_in_ref, w_out_ref,
    packed_ref, hidden_in_ref, raw_ref, embedding_ref,
):
    rows = history_ref[...].astype(F32)
    root = jnp.exp(jnp.log(jnp.abs(rows) * (1.0 / RANGE)) * (1.0 / 3.0)) * CODES
    codes = jnp.where(rows < 0.0, -root, root)
    packed_ref[0:TOK, :] = jnp.round(codes).astype(jnp.int32).astype(jnp.int16)
    wanted = wanted_ref[...]
    slot = lax.broadcasted_iota(jnp.int32, (2, WIDTH), 0)
    wanted = jnp.where(slot < counts_ref[...], wanted, -1)
    labels = jnp.concatenate([labels_ref[entry : entry + 1, :] for entry in range(4)], axis=1)
    at = lax.broadcasted_iota(jnp.int32, (16, WIDTH), 0)
    extras = jnp.where(at == 0, wanted[0:1], jnp.where(at == 1, wanted[1:2], labels))
    packed_ref[TOK:PACK_ROWS, :] = extras.astype(jnp.int16)

    hidden_in = dot(table_ref[...], w_in_ref[...])
    hidden_in_ref[...] = hidden_in
    raw = dot(silu(hidden_in).astype(BF), w_out_ref[...])
    raw_ref[...] = raw
    inv_norm = lax.rsqrt(jnp.sum(raw * raw, axis=-1, keepdims=True) + unit_eps)
    embedding_ref[...] = (raw * inv_norm).astype(BF)


def decode(codes):
    root = codes.astype(F32) * (RANGE ** (1.0 / 3.0) / CODES)
    return (root * root * root).astype(BF)


def tower_kernel(
    place_ref, packed_ref, w_in_ref, w_out_ref, user_ref, rows_ref, labels_ref,
    key_scr, value_scr, query_scr, total_scr,
):
    parity = place_ref[0]
    chip = place_ref[1]

    for block in range(CHIPS):
        extras = packed_ref[block, parity, TOK:PACK_ROWS, :].astype(F32)
        mine = pltpu.roll(extras, WIDTH - chip * 32, 1)
        rows_ref[block : block + 1, :] = mine[0:1, 0:TOK]
        rows_ref[CHIPS + block : CHIPS + block + 1, :] = mine[1:2, 0:TOK]
        labels_ref[block : block + 1, :] = extras[2:3]

    def project(step, carry):
        pieces = [packed_ref[2 * step + n // 2, n % 2, 0:TOK, :] for n in range(4)]
        rows = decode(jnp.concatenate(pieces, axis=0))
        at = pl.ds(pl.multiple_of(step * TILE, TILE), TILE)
        value_scr[at, :] = silu(dot(rows, w_in_ref[:, 512:1024])).astype(BF)
        key_scr[:, at] = silu(dot(w_in_ref[:, 1280:1536], rows, (((0,), (1,)), ((), ())))).astype(BF)
        return carry

    lax.fori_loop(0, 2 * HALF // TILE, project, 0)

    lane = lax.broadcasted_iota(jnp.int32, (TILE, 2 * DQK), 1)

    def tile(top, height, start, width, diagonal=None):
        if diagonal is not None:
            row = lax.broadcasted_iota(jnp.int32, (height, width), 0)
            key_at = lax.broadcasted_iota(jnp.int32, (height, width), 1) + diagonal[0]
            block = row // TOK + diagonal[1]
            allowed = key_at <= (2 * block + parity) * TOK + row % TOK
        weights = []
        for head in range(HEADS):
            keys = key_scr[(head // 2) * 2 * DQK : (head // 2 + 1) * 2 * DQK, pl.ds(start, width)]
            weight = half_silu(dot(query_scr[head, top : top + height], keys))
            if diagonal is not None:
                weight = jnp.where(allowed, weight, 0.0)
            weights.append(weight.astype(BF))
        for head in range(HEADS):
            values = value_scr[pl.ds(start, width), head * 128 : (head + 1) * 128]
            total_scr[top : top + height, head * 128 : (head + 1) * 128] += dot(weights[head], values)

    for group in range(HALF // TILE):
        rows = decode(
            jnp.concatenate(
                [packed_ref[4 * group + n, parity, 0:TOK, :] for n in range(4)], axis=0
            )
        )
        query = (silu(dot(rows, w_in_ref[:, 1024:1280])).astype(BF) * 0.0625).astype(BF)
        for head in range(HEADS):
            both = query[:, (head // 2) * 2 * DQK : (head // 2 + 1) * 2 * DQK]
            mine = (lane >= DQK) if head % 2 else (lane < DQK)
            query_scr[head] = jnp.where(mine, both, jnp.zeros_like(both))
        total_scr[...] = jnp.zeros_like(total_scr)
        base = group * 2 * TILE

        def earlier(step, carry):
            tile(0, TILE, pl.multiple_of(step * TILE, TILE), TILE)
            return carry

        lax.fori_loop(0, base // TILE, earlier, 0)
        for pair in range(2):
            top = pair * 2 * TOK
            first = base + 2 * top
            if pair:
                tile(top, 2 * TOK, base, TILE)
            tile(top, 2 * TOK, first, 2 * TOK, (0, 0))
            tile(top + TOK, TOK, first + 2 * TOK, 2 * TOK, (2 * TOK, 1))

        attended = total_scr[...]
        centered = attended - jnp.mean(attended, axis=-1, keepdims=True)
        variance = jnp.mean(centered * centered, axis=-1, keepdims=True)
        normed = centered * lax.rsqrt(variance + norm_eps)
        gate_units = silu(dot(rows, w_in_ref[:, 0:512]))
        mixed_rows = (normed * gate_units).astype(BF)
        updated = rows.astype(F32) + dot(mixed_rows, w_out_ref[...])
        scale = lax.rsqrt(jnp.sum(updated * updated, axis=-1, keepdims=True) + unit_eps)
        user_ref[group * TILE : (group + 1) * TILE, :] = (updated * scale).astype(BF)


def label_places(labels_ref, block, entry, chip):
    label = labels_ref[block : block + 1, entry * TOK : (entry + 1) * TOK].astype(jnp.int32)
    local = label - chip * 64
    inside = (label >= 0) & (local >= 0) & (local < 64)
    return jnp.where(inside, (local & 1) * 32 + (local >> 1), -1)


def scores_kernel(
    place_ref, table_ref, user_ref, rows_ref, labels_ref,
    exps_ref, hits_ref, exchange_ref, entry_scr,
):
    chip = place_ref[1]
    row_ids = lax.broadcasted_iota(jnp.int32, (32, TOK), 1).astype(F32)
    for owner in range(32):
        asked = jnp.broadcast_to(rows_ref[:, owner : owner + 1], (32, TOK))
        rows = dot((row_ids == asked).astype(BF), table_ref[owner * TOK : (owner + 1) * TOK, :])
        used = (asked >= 0.0).astype(F32)
        for slot in range(2):
            entry_scr[4, pl.ds(slot * 32 + owner, 16, stride=64), :] = used[
                slot * 16 : (slot + 1) * 16
            ]
            for part in range(4):
                entry_scr[part, pl.ds(slot * 32 + owner, 16, stride=64), :] = rows[
                    slot * 16 : (slot + 1) * 16, part * 128 : (part + 1) * 128
                ]
    slot_ids = lax.broadcasted_iota(jnp.int32, (64, TOK), 0)
    exchange_ref[...] = jnp.zeros_like(exchange_ref)
    for block in range(CHIPS):
        entries = jnp.concatenate(
            [entry_scr[part, block * 64 : (block + 1) * 64, :] for part in range(4)], axis=1
        ).astype(BF)
        scores = dot(entries, user_ref[block * TOK : (block + 1) * TOK, :], NT) * inverse_sharpness
        used = entry_scr[4, block * 64 : (block + 1) * 64, :] > 0.0
        exps = jnp.where(used, jnp.exp(scores), 0.0)
        exps_ref[block] = exps
        hits = jnp.zeros((64, TOK), F32)
        for entry in range(4):
            place = label_places(labels_ref, block, entry, chip)
            hits = hits + (slot_ids == place).astype(F32)
        hits_ref[block] = hits
        total = jnp.sum(exps, axis=0, keepdims=True)
        exchange_ref[:, block : block + 1, :] = jnp.broadcast_to(total[None], (CHIPS, 1, TOK))
        exchange_ref[block, 16:17, :] = jnp.sum(hits * scores, axis=0, keepdims=True)


def gradient_kernel(
    place_ref, exps_ref, hits_ref, user_ref, exchange_ref, labels_ref, rows_ref,
    send_ref, loss_ref, grad_scr,
):
    chip = place_ref[1]
    sums = jnp.sum(exchange_ref[...], axis=0)
    positives = jnp.zeros((CHIPS, TOK), F32)
    for entry in range(4):
        positives = positives + (labels_ref[:, entry * TOK : (entry + 1) * TOK] >= 0.0).astype(F32)
    divisor = jnp.maximum(positives, 1.0)
    totals = sums[0:16]
    own = lax.broadcasted_iota(jnp.int32, (CHIPS, TOK), 0) == chip
    losses = (positives * jnp.log(totals) - sums[16:17]) / divisor
    loss_ref[...] = jnp.sum(jnp.where(own, losses, 0.0), axis=0, keepdims=True)
    exp_scale = positives / (divisor * totals)
    hit_scale = 1.0 / divisor
    for block in range(CHIPS):
        score_grad = (
            exps_ref[block] * exp_scale[block : block + 1]
            - hits_ref[block] * hit_scale[block : block + 1]
        ).astype(BF)
        grads = dot(score_grad, user_ref[block * TOK : (block + 1) * TOK, :]) * inverse_sharpness
        for slot in range(2):
            for part in range(4):
                at = part * 32 + slot * 16 + block
                grad_scr[pl.ds(at, 32, stride=SEND_ROWS), :] = grads[
                    slot * 32 : (slot + 1) * 32, part * 128 : (part + 1) * 128
                ]
    at = lax.broadcasted_iota(jnp.int32, (32, TOK), 0) + (place_ref[2] & 3) * 32
    spread = (lax.broadcasted_iota(jnp.int32, (32, TOK), 1) == at).astype(BF)
    index = dot(rows_ref[...].astype(BF), spread, (((0,), (0,)), ((), ())))[0:32]
    zeros = jnp.zeros((32, TOK), F32)
    for extra in range(8):
        grad_scr[pl.ds(TOK + extra, 32, stride=SEND_ROWS), :] = zeros if extra else index
    send_ref[...] = grad_scr[...].astype(BF)


def owner_kernel(
    arrived_ref, index_ref, hidden_in_ref, raw_ref, w_in_ref, w_out_ref, gradient_ref, rows_scr
):
    row_ids = lax.broadcasted_iota(jnp.int32, (TOK, TOK), 0).astype(F32)
    row_grad = jnp.zeros((TOK, WIDTH), F32)
    for group in range(8):
        index = jnp.zeros((1, TOK), F32)
        for member in range(4):
            sender = group * 4 + member
            index = index + index_ref[sender : sender + 1, :]
            for part in range(4):
                rows_scr[member * 32 : (member + 1) * 32, part * 128 : (part + 1) * 128] = arrived_ref[
                    sender, part * 32 : (part + 1) * 32, :
                ]
        pick = (row_ids == index).astype(BF)
        row_grad = row_grad + dot(pick, rows_scr[...])
    raw = raw_ref[...]
    inv_norm = lax.rsqrt(jnp.sum(raw * raw, axis=-1, keepdims=True) + unit_eps)
    unit = raw * inv_norm
    raw_grad = (row_grad - unit * jnp.sum(unit * row_grad, axis=-1, keepdims=True)) * inv_norm
    hidden_grad = split_product(raw_grad, w_out_ref[...])
    hidden_in = hidden_in_ref[...]
    sigma = 0.5 * jnp.tanh(0.5 * hidden_in) + 0.5
    input_grad = hidden_grad * (sigma * (1.0 + hidden_in * (1.0 - sigma)))
    gradient_ref[...] = split_product(input_grad, w_in_ref[...])


def on_device(
    history, w_in, w_out, item_table, w_item_in, w_item_out, req_rows, req_counts, labels
):
    chip = lax.axis_index("z")
    core = lax.axis_index("core")
    place = jnp.stack([core, chip, lax.axis_index("item")]).astype(jnp.int32)

    with jax.named_scope("prepare"):
        packed, hidden_in, raw_embed, embedding = call(
            prepare_kernel,
            (
                jax.ShapeDtypeStruct((PACK_ROWS, WIDTH), jnp.int16),
                jax.ShapeDtypeStruct((TOK, HIDDEN), F32),
                jax.ShapeDtypeStruct((TOK, WIDTH), F32),
                jax.ShapeDtypeStruct((TOK, WIDTH), BF),
            ),
            0,
            7,
        )(
            history[0], req_rows[0, 0].T, req_counts[0], labels[0].T,
            item_table, w_item_in, w_item_out,
        )

    with jax.named_scope("table_gather"):
        table = lax.all_gather(embedding, ("core", "item"), axis=0, tiled=True)

    with jax.named_scope("history_gather"):
        gathered = lax.all_gather(packed, ("z", "core"), axis=0, tiled=True)

    with jax.named_scope("tower"):
        user_rows, asked_rows, label_rows = call(
            tower_kernel,
            (
                jax.ShapeDtypeStruct((HALF, WIDTH), BF),
                jax.ShapeDtypeStruct((32, TOK), F32),
                jax.ShapeDtypeStruct((CHIPS, WIDTH), F32),
            ),
            1,
            3,
            [
                pltpu.VMEM((HEADS * DQK, 2 * HALF), BF),
                pltpu.VMEM((2 * HALF, WIDTH), BF),
                pltpu.VMEM((HEADS, TILE, 2 * DQK), BF),
                pltpu.VMEM((TILE, WIDTH), F32),
            ],
        )(place, gathered.reshape(CHIPS, 2, PACK_ROWS, WIDTH), w_in, w_out)

    with jax.named_scope("scores"):
        exps, hits, exchange = call(
            scores_kernel,
            (
                jax.ShapeDtypeStruct((CHIPS, 64, TOK), F32),
                jax.ShapeDtypeStruct((CHIPS, 64, TOK), F32),
                jax.ShapeDtypeStruct((CHIPS, 24, TOK), F32),
            ),
            1,
            4,
            [pltpu.VMEM((5, 1024, 128), F32)],
        )(place, table, user_rows, asked_rows, label_rows)

    with jax.named_scope("totals_exchange"):
        exchange = lax.all_to_all(exchange, "z", split_axis=0, concat_axis=0, tiled=True)

    with jax.named_scope("gradient_rows"):
        send, loss = call(
            gradient_kernel,
            (
                jax.ShapeDtypeStruct((32 * SEND_ROWS, 128), BF),
                jax.ShapeDtypeStruct((1, TOK), F32),
            ),
            1,
            6,
            [pltpu.VMEM((32 * SEND_ROWS, 128), F32)],
        )(place, exps, hits, user_rows, exchange, label_rows, asked_rows)

    with jax.named_scope("gradient_send"):
        arrived = lax.all_to_all(
            send.reshape(32, SEND_ROWS, 128), ("core", "item"), split_axis=0, concat_axis=0, tiled=True
        )

    with jax.named_scope("owner"):
        gradient = call(
            owner_kernel,
            jax.ShapeDtypeStruct((TOK, WIDTH), F32),
            0,
            6,
            [pltpu.VMEM((TOK, WIDTH), BF)],
        )(arrived, arrived[:, TOK].astype(F32), hidden_in, raw_embed, w_item_in, w_item_out)
    return (loss, gradient)


def solution(mesh):
    split = Mesh(mesh.devices.reshape(CHIPS, 2, 16), ("z", "core", "item"))
    rows = ("z", "core")
    placed = (
        P("item", rows, None),
        P(),
        P(),
        P(("z", "core", "item"), None),
        P(),
        P(),
        P("item", rows, None, None),
        P("item", rows, None),
        P("item", rows, None),
    )
    return jax.shard_map(
        on_device,
        mesh=split,
        in_specs=placed,
        out_specs=(P("item", rows), P(("z", "core", "item"), None)),
        check_vma=False,
    )
```

```python
import jax
import jax.numpy as jnp
from jax import lax
from jax.experimental import pallas as pl
from jax.experimental.pallas import tpu as pltpu
from jax.sharding import Mesh
from jax.sharding import PartitionSpec as P

HEADS = 4
DQK = 64
TOK = 128
WIDTH = 512
HIDDEN = 1024
CHIPS = 16
ITEMS = 16
HALF = CHIPS * TOK
TILE = 512
PACK_ROWS = 144
SEND_ROWS = 136
RANGE = 6.0
CODES = 32760.0

inverse_sharpness = 50.0
norm_eps = 1e-05
unit_eps = 1e-06

BF = jnp.bfloat16
F32 = jnp.float32
VMEM_LIMIT = 56 * 1024 * 1024

NN = (((1,), (0,)), ((), ()))
NT = (((1,), (1,)), ((), ()))


def dot(left, right, contract=NN):
    return lax.dot_general(left, right, contract, preferred_element_type=F32)


def half_silu(half):
    return half + half * jnp.tanh(half)


def silu(inputs):
    return half_silu(0.5 * inputs)


def split_product(left, weight):
    high = left.astype(BF)
    low = (left - high.astype(F32)).astype(BF)
    return dot(high, weight, NT) + dot(low, weight, NT)


def call(kernel, out_shape, inputs, scratch=()):
    space = [pl.BlockSpec(memory_space=pltpu.VMEM)] * inputs
    return pl.pallas_call(
        kernel,
        out_shape=out_shape,
        in_specs=space,
        out_specs=jax.tree.map(lambda _: pl.BlockSpec(memory_space=pltpu.VMEM), out_shape),
        scratch_shapes=list(scratch),
        compiler_params=pltpu.CompilerParams(vmem_limit_bytes=VMEM_LIMIT),
    )


def prepare_kernel(
    history_ref, wanted_ref, counts_ref, labels_ref, table_ref, w_in_ref, w_out_ref,
    packed_ref, hidden_in_ref, raw_ref, copies_ref,
):
    rows = history_ref[...].astype(F32)
    root = jnp.exp(jnp.log(jnp.abs(rows) * (1.0 / RANGE)) * (1.0 / 3.0)) * CODES
    codes = jnp.where(rows < 0.0, -root, root)
    packed_ref[0:TOK, :] = jnp.round(codes).astype(jnp.int32).astype(jnp.int16)
    wanted = wanted_ref[...]
    slot = lax.broadcasted_iota(jnp.int32, (2, WIDTH), 0)
    wanted = jnp.where(slot < counts_ref[...], wanted, -1)
    labels = jnp.concatenate([labels_ref[entry : entry + 1, :] for entry in range(4)], axis=1)
    at = lax.broadcasted_iota(jnp.int32, (16, WIDTH), 0)
    extras = jnp.where(at == 0, wanted[0:1], jnp.where(at == 1, wanted[1:2], labels))
    packed_ref[TOK:PACK_ROWS, :] = extras.astype(jnp.int16)

    hidden_in = dot(table_ref[...], w_in_ref[...])
    hidden_in_ref[...] = hidden_in
    raw = dot(silu(hidden_in).astype(BF), w_out_ref[...])
    raw_ref[...] = raw
    inv_norm = lax.rsqrt(jnp.sum(raw * raw, axis=-1, keepdims=True) + unit_eps)
    embedding = (raw * inv_norm).astype(BF)
    for rank in range(ITEMS):
        copies_ref[rank] = embedding


def decode(codes):
    root = codes.astype(F32) * (RANGE ** (1.0 / 3.0) / CODES)
    return (root * root * root).astype(BF)


def tower_kernel(
    packed_ref, w_in_ref, w_out_ref, user_ref, rows_ref, labels_ref,
    key_scr, value_scr, query_scr, total_scr,
):
    parity = lax.axis_index("core")
    chip = lax.axis_index("z")

    first = lax.broadcasted_iota(jnp.int32, (16, WIDTH), 1) < ITEMS
    near = WIDTH - chip * 32 - parity * ITEMS
    far = lax.rem(WIDTH + ITEMS - chip * 32 - (1 - parity) * ITEMS, WIDTH)
    for block in range(CHIPS):
        extras = packed_ref[block, parity, TOK:PACK_ROWS, :].astype(F32)
        mine = jnp.where(first, pltpu.roll(extras, near, 1), pltpu.roll(extras, far, 1))
        rows_ref[block : block + 1, :] = mine[0:1, 0:TOK]
        rows_ref[CHIPS + block : CHIPS + block + 1, :] = mine[1:2, 0:TOK]
        labels_ref[block : block + 1, :] = extras[2:3]

    def project(step, carry):
        pieces = [packed_ref[2 * step + n // 2, n % 2, 0:TOK, :] for n in range(4)]
        rows = decode(jnp.concatenate(pieces, axis=0))
        at = pl.ds(pl.multiple_of(step * TILE, TILE), TILE)
        value_scr[at, :] = silu(dot(rows, w_in_ref[:, 512:1024])).astype(BF)
        key_scr[:, at] = silu(dot(w_in_ref[:, 1280:1536], rows, (((0,), (1,)), ((), ())))).astype(BF)
        return carry

    lax.fori_loop(0, 2 * HALF // TILE, project, 0)

    lane = lax.broadcasted_iota(jnp.int32, (TILE, 2 * DQK), 1)

    def tile(top, height, start, width, diagonal=None):
        if diagonal is not None:
            row = lax.broadcasted_iota(jnp.int32, (height, width), 0)
            key_at = lax.broadcasted_iota(jnp.int32, (height, width), 1) + diagonal[0]
            block = row // TOK + diagonal[1]
            allowed = key_at <= (2 * block + parity) * TOK + row % TOK
        weights = []
        for head in range(HEADS):
            keys = key_scr[(head // 2) * 2 * DQK : (head // 2 + 1) * 2 * DQK, pl.ds(start, width)]
            weight = half_silu(dot(query_scr[head, top : top + height], keys))
            if diagonal is not None:
                weight = jnp.where(allowed, weight, 0.0)
            weights.append(weight.astype(BF))
        for head in range(HEADS):
            values = value_scr[pl.ds(start, width), head * 128 : (head + 1) * 128]
            total_scr[top : top + height, head * 128 : (head + 1) * 128] += dot(weights[head], values)

    for group in range(HALF // TILE):
        rows = decode(
            jnp.concatenate(
                [packed_ref[4 * group + n, parity, 0:TOK, :] for n in range(4)], axis=0
            )
        )
        query = (silu(dot(rows, w_in_ref[:, 1024:1280])).astype(BF) * 0.0625).astype(BF)
        for head in range(HEADS):
            both = query[:, (head // 2) * 2 * DQK : (head // 2 + 1) * 2 * DQK]
            mine = (lane >= DQK) if head % 2 else (lane < DQK)
            query_scr[head] = jnp.where(mine, both, jnp.zeros_like(both))
        total_scr[...] = jnp.zeros_like(total_scr)
        base = group * 2 * TILE

        def earlier(step, carry):
            tile(0, TILE, pl.multiple_of(step * TILE, TILE), TILE)
            return carry

        lax.fori_loop(0, base // TILE, earlier, 0)
        for pair in range(2):
            top = pair * 2 * TOK
            first = base + 2 * top
            if pair:
                tile(top, 2 * TOK, base, TILE)
            tile(top, 2 * TOK, first, 2 * TOK, (0, 0))
            tile(top + TOK, TOK, first + 2 * TOK, 2 * TOK, (2 * TOK, 1))

        attended = total_scr[...]
        centered = attended - jnp.mean(attended, axis=-1, keepdims=True)
        variance = jnp.mean(centered * centered, axis=-1, keepdims=True)
        normed = centered * lax.rsqrt(variance + norm_eps)
        gate_units = silu(dot(rows, w_in_ref[:, 0:512]))
        mixed_rows = (normed * gate_units).astype(BF)
        updated = rows.astype(F32) + dot(mixed_rows, w_out_ref[...])
        scale = lax.rsqrt(jnp.sum(updated * updated, axis=-1, keepdims=True) + unit_eps)
        user_ref[group * TILE : (group + 1) * TILE, :] = (updated * scale).astype(BF)


def label_places(labels_ref, block, entry, chip, core):
    label = labels_ref[block : block + 1, entry * TOK : (entry + 1) * TOK].astype(jnp.int32)
    local = label - chip * 64
    inside = (label >= 0) & (local >= 0) & (local < 64)
    return jnp.where(inside, (local & 1) * 32 + ((local >> 1) ^ (core * ITEMS)), -1)


def scores_kernel(
    near_ref, far_ref, user_ref, rows_ref, labels_ref,
    exps_ref, hits_ref, exchange_ref, entry_scr,
):
    chip = lax.axis_index("z")
    core = lax.axis_index("core")
    row_ids = lax.broadcasted_iota(jnp.int32, (32, TOK), 1).astype(F32)
    for owner in range(32):
        asked = jnp.broadcast_to(rows_ref[:, owner : owner + 1], (32, TOK))
        table = (far_ref if owner // ITEMS else near_ref)[owner % ITEMS]
        rows = dot((row_ids == asked).astype(BF), table)
        used = (asked >= 0.0).astype(F32)
        for slot in range(2):
            entry_scr[4, pl.ds(slot * 32 + owner, 16, stride=64), :] = used[
                slot * 16 : (slot + 1) * 16
            ]
            for part in range(4):
                entry_scr[part, pl.ds(slot * 32 + owner, 16, stride=64), :] = rows[
                    slot * 16 : (slot + 1) * 16, part * 128 : (part + 1) * 128
                ]
    slot_ids = lax.broadcasted_iota(jnp.int32, (64, TOK), 0)
    exchange_ref[...] = jnp.zeros_like(exchange_ref)
    for block in range(CHIPS):
        entries = jnp.concatenate(
            [entry_scr[part, block * 64 : (block + 1) * 64, :] for part in range(4)], axis=1
        ).astype(BF)
        scores = dot(entries, user_ref[block * TOK : (block + 1) * TOK, :], NT) * inverse_sharpness
        used = entry_scr[4, block * 64 : (block + 1) * 64, :] > 0.0
        exps = jnp.where(used, jnp.exp(scores), 0.0)
        exps_ref[block] = exps
        hits = jnp.zeros((64, TOK), F32)
        for entry in range(4):
            place = label_places(labels_ref, block, entry, chip, core)
            hits = hits + (slot_ids == place).astype(F32)
        hits_ref[block] = hits
        total = jnp.sum(exps, axis=0, keepdims=True)
        exchange_ref[:, block : block + 1, :] = jnp.broadcast_to(total[None], (CHIPS, 1, TOK))
        exchange_ref[block, 16:17, :] = jnp.sum(hits * scores, axis=0, keepdims=True)


def gradient_kernel(
    exps_ref, hits_ref, user_ref, exchange_ref, labels_ref, rows_ref,
    near_ref, far_ref, loss_ref, near_scr, far_scr,
):
    chip = lax.axis_index("z")
    sides = (near_scr, far_scr)
    sums = jnp.sum(exchange_ref[...], axis=0)
    positives = jnp.zeros((CHIPS, TOK), F32)
    for entry in range(4):
        positives = positives + (labels_ref[:, entry * TOK : (entry + 1) * TOK] >= 0.0).astype(F32)
    divisor = jnp.maximum(positives, 1.0)
    totals = sums[0:16]
    own = lax.broadcasted_iota(jnp.int32, (CHIPS, TOK), 0) == chip
    losses = (positives * jnp.log(totals) - sums[16:17]) / divisor
    loss_ref[...] = jnp.sum(jnp.where(own, losses, 0.0), axis=0, keepdims=True)
    exp_scale = positives / (divisor * totals)
    hit_scale = 1.0 / divisor
    for block in range(CHIPS):
        score_grad = (
            exps_ref[block] * exp_scale[block : block + 1]
            - hits_ref[block] * hit_scale[block : block + 1]
        ).astype(BF)
        grads = dot(score_grad, user_ref[block * TOK : (block + 1) * TOK, :]) * inverse_sharpness
        for slot in range(2):
            for part in range(4):
                for side in range(2):
                    at = part * 32 + slot * 16 + block
                    first = slot * 32 + side * 16
                    sides[side][pl.ds(at, 16, stride=SEND_ROWS), :] = grads[
                        first : first + 16, part * 128 : (part + 1) * 128
                    ]
    at = lax.broadcasted_iota(jnp.int32, (32, TOK), 0) + (lax.axis_index("item") & 3) * 32
    spread = (lax.broadcasted_iota(jnp.int32, (32, TOK), 1) == at).astype(BF)
    index = dot(rows_ref[...].astype(BF), spread, (((0,), (0,)), ((), ())))[0:32]
    zeros = jnp.zeros((16, TOK), F32)
    for side in range(2):
        for extra in range(8):
            rows = zeros if extra else index[side * 16 : (side + 1) * 16]
            sides[side][pl.ds(TOK + extra, 16, stride=SEND_ROWS), :] = rows
    near_ref[...] = near_scr[...].astype(BF)
    far_ref[...] = far_scr[...].astype(BF)


def owner_kernel(
    arrived_ref, hidden_in_ref, raw_ref, w_in_ref, w_out_ref, gradient_ref, rows_scr
):
    row_ids = lax.broadcasted_iota(jnp.int32, (TOK, TOK), 0).astype(F32)
    row_grad = jnp.zeros((TOK, WIDTH), F32)
    for group in range(4):
        extras = jnp.zeros((16, TOK), F32)
        for member in range(4):
            sender = group * 4 + member
            extras = extras + arrived_ref[sender, 2 * TOK :, :].astype(F32)
            for side in range(2):
                for part in range(4):
                    first = side * TOK + part * 32
                    rows_scr[
                        side * TOK + member * 32 : side * TOK + (member + 1) * 32,
                        part * 128 : (part + 1) * 128,
                    ] = arrived_ref[sender, first : first + 32, :]
        index = jnp.concatenate([extras[0:1], extras[8:9]], axis=1)
        pick = (jnp.concatenate([row_ids, row_ids], axis=1) == index).astype(BF)
        row_grad = row_grad + dot(pick, rows_scr[...])
    raw = raw_ref[...]
    inv_norm = lax.rsqrt(jnp.sum(raw * raw, axis=-1, keepdims=True) + unit_eps)
    unit = raw * inv_norm
    raw_grad = (row_grad - unit * jnp.sum(unit * row_grad, axis=-1, keepdims=True)) * inv_norm
    hidden_grad = split_product(raw_grad, w_out_ref[...])
    hidden_in = hidden_in_ref[...]
    sigma = 0.5 * jnp.tanh(0.5 * hidden_in) + 0.5
    input_grad = hidden_grad * (sigma * (1.0 + hidden_in * (1.0 - sigma)))
    gradient_ref[...] = split_product(input_grad, w_in_ref[...])


def on_device(
    history, w_in, w_out, item_table, w_item_in, w_item_out, req_rows, req_counts, labels
):
    swap = [(0, 1), (1, 0)]

    with jax.named_scope("prepare"):
        packed, hidden_in, raw_embed, copies = call(
            prepare_kernel,
            (
                jax.ShapeDtypeStruct((PACK_ROWS, WIDTH), jnp.int16),
                jax.ShapeDtypeStruct((TOK, HIDDEN), F32),
                jax.ShapeDtypeStruct((TOK, WIDTH), F32),
                jax.ShapeDtypeStruct((ITEMS, TOK, WIDTH), BF),
            ),
            7,
        )(
            history[0], req_rows[0, 0].T, req_counts[0], labels[0].T,
            item_table, w_item_in, w_item_out,
        )

    with jax.named_scope("table_gather"):
        near_table = lax.all_to_all(copies, "item", split_axis=0, concat_axis=0, tiled=True)

    with jax.named_scope("history_gather"):
        gathered = lax.all_gather(packed, ("z", "core"), axis=0, tiled=True)
        gathered, near_table = lax.optimization_barrier((gathered, near_table))

    with jax.named_scope("table_swap"):
        far_table = lax.ppermute(near_table, "core", swap)

    with jax.named_scope("tower"):
        user_rows, asked_rows, label_rows = call(
            tower_kernel,
            (
                jax.ShapeDtypeStruct((HALF, WIDTH), BF),
                jax.ShapeDtypeStruct((32, TOK), F32),
                jax.ShapeDtypeStruct((CHIPS, WIDTH), F32),
            ),
            3,
            [
                pltpu.VMEM((HEADS * DQK, 2 * HALF), BF),
                pltpu.VMEM((2 * HALF, WIDTH), BF),
                pltpu.VMEM((HEADS, TILE, 2 * DQK), BF),
                pltpu.VMEM((TILE, WIDTH), F32),
            ],
        )(gathered.reshape(CHIPS, 2, PACK_ROWS, WIDTH), w_in, w_out)

    with jax.named_scope("scores"):
        exps, hits, exchange = call(
            scores_kernel,
            (
                jax.ShapeDtypeStruct((CHIPS, 64, TOK), F32),
                jax.ShapeDtypeStruct((CHIPS, 64, TOK), F32),
                jax.ShapeDtypeStruct((CHIPS, 24, TOK), F32),
            ),
            5,
            [pltpu.VMEM((5, 1024, 128), F32)],
        )(near_table, far_table, user_rows, asked_rows, label_rows)

    with jax.named_scope("totals_exchange"):
        exchange = lax.all_to_all(exchange, "z", split_axis=0, concat_axis=0, tiled=True)

    with jax.named_scope("gradient_rows"):
        near, far, loss = call(
            gradient_kernel,
            (
                jax.ShapeDtypeStruct((ITEMS * SEND_ROWS, 128), BF),
                jax.ShapeDtypeStruct((ITEMS * SEND_ROWS, 128), BF),
                jax.ShapeDtypeStruct((1, TOK), F32),
            ),
            6,
            [pltpu.VMEM((ITEMS * SEND_ROWS, 128), F32)] * 2,
        )(exps, hits, user_rows, exchange, label_rows, asked_rows)

    with jax.named_scope("gradient_swap"):
        near = near.reshape(ITEMS, SEND_ROWS, 128)
        far = lax.ppermute(far.reshape(ITEMS, SEND_ROWS, 128), "core", swap)
        send = jnp.concatenate([near[:, :TOK], far[:, :TOK], near[:, TOK:], far[:, TOK:]], axis=1)

    with jax.named_scope("gradient_send"):
        arrived = lax.all_to_all(send, "item", split_axis=0, concat_axis=0, tiled=True)

    with jax.named_scope("owner"):
        gradient = call(
            owner_kernel,
            jax.ShapeDtypeStruct((TOK, WIDTH), F32),
            5,
            [pltpu.VMEM((2 * TOK, WIDTH), BF)],
        )(arrived, hidden_in, raw_embed, w_item_in, w_item_out)
    return (loss, gradient)


def solution(mesh):
    split = Mesh(mesh.devices.reshape(CHIPS, 2, 16), ("z", "core", "item"))
    rows = ("z", "core")
    placed = (
        P("item", rows, None),
        P(),
        P(),
        P(("z", "core", "item"), None),
        P(),
        P(),
        P("item", rows, None, None),
        P("item", rows, None),
        P("item", rows, None),
    )
    return jax.shard_map(
        on_device,
        mesh=split,
        in_specs=placed,
        out_specs=(P("item", rows), P(("z", "core", "item"), None)),
        check_vma=False,
    )
```

```python
import jax
import jax.numpy as jnp
from jax import lax
from jax.experimental import pallas as pl
from jax.experimental.pallas import tpu as pltpu
from jax.sharding import Mesh
from jax.sharding import PartitionSpec as P

HEADS = 4
DQK = 64
TOK = 128
WIDTH = 512
HIDDEN = 1024
CHIPS = 16
HALF = CHIPS * TOK
TILE = 512
PACK_ROWS = 528
SEND_ROWS = 144
RANGE = 6.0
CODES = 32760.0

inverse_sharpness = 50.0
norm_eps = 1e-05
unit_eps = 1e-06

BF = jnp.bfloat16
F32 = jnp.float32
VMEM_LIMIT = 56 * 1024 * 1024

NN = (((1,), (0,)), ((), ()))
NT = (((1,), (1,)), ((), ()))


def dot(left, right, contract=NN):
    return lax.dot_general(left, right, contract, preferred_element_type=F32)


def half_silu(half):
    return half + half * jnp.tanh(half)


def silu(inputs):
    return half_silu(0.5 * inputs)


def split_product(left, weight):
    high = left.astype(BF)
    low = (left - high.astype(F32)).astype(BF)
    return dot(high, weight, NT) + dot(low, weight, NT)


def call(kernel, out_shape, spaces, scratch=()):
    kinds = {"v": pltpu.VMEM, "h": pl.ANY}
    return pl.pallas_call(
        kernel,
        out_shape=out_shape,
        in_specs=[pl.BlockSpec(memory_space=kinds[space]) for space in spaces],
        out_specs=jax.tree.map(lambda _: pl.BlockSpec(memory_space=pltpu.VMEM), out_shape),
        scratch_shapes=list(scratch),
        compiler_params=pltpu.CompilerParams(vmem_limit_bytes=VMEM_LIMIT),
    )


def prepare_kernel(
    history_ref, wanted_ref, counts_ref, labels_ref, table_ref, w_in_ref, w_out_ref,
    packed_ref, hidden_in_ref, raw_ref, copies_ref,
):
    rows = history_ref[...].astype(F32)
    root = jnp.exp(jnp.log(jnp.abs(rows) * (1.0 / RANGE)) * (1.0 / 3.0)) * CODES
    codes = jnp.where(rows < 0.0, -root, root)
    codes = jnp.round(codes).astype(jnp.int32).astype(jnp.int16)
    for part in range(4):
        packed_ref[part * TOK : (part + 1) * TOK, :] = codes[:, part * 128 : (part + 1) * 128]
    wanted = wanted_ref[...]
    slot = lax.broadcasted_iota(jnp.int32, (2, WIDTH), 0)
    wanted = jnp.where(slot < counts_ref[...], wanted, -1)
    extras = [
        wanted[slot : slot + 1, part * 128 : (part + 1) * 128] for slot in range(2) for part in range(4)
    ]
    extras += [labels_ref[...], jnp.zeros((4, TOK), jnp.int32)]
    packed_ref[WIDTH:PACK_ROWS, :] = jnp.concatenate(extras, axis=0).astype(jnp.int16)

    hidden_in = dot(table_ref[...], w_in_ref[...])
    hidden_in_ref[...] = hidden_in
    raw = dot(silu(hidden_in).astype(BF), w_out_ref[...])
    raw_ref[...] = raw
    inv_norm = lax.rsqrt(jnp.sum(raw * raw, axis=-1, keepdims=True) + unit_eps)
    embedding = (raw * inv_norm).astype(BF)
    for rank in range(32):
        copies_ref[rank] = embedding


def decode(codes):
    root = codes.astype(F32) * (RANGE ** (1.0 / 3.0) / CODES)
    return (root * root * root).astype(BF)


def rank_of(owner):
    return (owner % 16) * 2 + owner // 16


def label_places(labels_ref, block, entry, chip):
    label = labels_ref[block : block + 1, entry * TOK : (entry + 1) * TOK].astype(jnp.int32)
    local = label - chip * 64
    inside = (label >= 0) & (local >= 0) & (local < 64)
    return jnp.where(inside, (local & 1) * 32 + (local >> 1), -1)


def block_rows(packed_ref, chip, core):
    parts = [packed_ref[chip, core, part * TOK : (part + 1) * TOK, :] for part in range(4)]
    return jnp.concatenate(parts, axis=1)


def tower_kernel(
    packed_ref, w_in_ref, w_out_ref, table_hbm,
    user_ref, exps_ref, hits_ref, exchange_ref, rows_ref, labels_ref,
    key_scr, value_scr, query_scr, total_scr, entry_scr, table_scr, table_sem,
):
    parity = lax.axis_index("core")
    chip = lax.axis_index("z")
    table_copy = pltpu.make_async_copy(table_hbm, table_scr, table_sem)
    table_copy.start()

    shift = TOK - lax.rem(chip, 4) * 32
    row_at = lax.broadcasted_iota(jnp.int32, (16, TOK), 0)
    chip_row = lax.div(chip, 4)
    for block in range(CHIPS):
        extras = packed_ref[block, parity, WIDTH:PACK_ROWS, :].astype(F32)
        mine = pltpu.roll(extras, shift, 1)
        for slot in range(2):
            chosen = jnp.where(row_at == chip_row + 4 * slot, mine, 0.0)
            at = slot * CHIPS + block
            rows_ref[at : at + 1, :] = jnp.sum(chosen, axis=0, keepdims=True)
        labels_ref[block : block + 1, :] = jnp.concatenate(
            [extras[8 + entry : 9 + entry] for entry in range(4)], axis=1
        )

    def project(step):
        pieces = [block_rows(packed_ref, 2 * step + n // 2, n % 2) for n in range(4)]
        rows = decode(jnp.concatenate(pieces, axis=0))
        at = slice(step * TILE, (step + 1) * TILE)
        value_scr[at, :] = silu(dot(rows, w_in_ref[:, 512:1024])).astype(BF)
        key_scr[:, at] = silu(dot(w_in_ref[:, 1280:1536], rows, (((0,), (1,)), ((), ())))).astype(BF)

    lane = lax.broadcasted_iota(jnp.int32, (TILE, 2 * DQK), 1)

    def tile(top, height, start, width, diagonal=None):
        if diagonal is not None:
            row = lax.broadcasted_iota(jnp.int32, (height, width), 0)
            key_at = lax.broadcasted_iota(jnp.int32, (height, width), 1) + diagonal[0]
            block = row // TOK + diagonal[1]
            allowed = key_at <= (2 * block + parity) * TOK + row % TOK
        weights = []
        for head in range(HEADS):
            keys = key_scr[(head // 2) * 2 * DQK : (head // 2 + 1) * 2 * DQK, start : start + width]
            weight = half_silu(dot(query_scr[head, top : top + height], keys))
            if diagonal is not None:
                weight = jnp.where(allowed, weight, 0.0)
            weights.append(weight.astype(BF))
        for head in range(HEADS):
            values = value_scr[start : start + width, head * 128 : (head + 1) * 128]
            total_scr[top : top + height, head * 128 : (head + 1) * 128] += dot(weights[head], values)

    for group in range(HALF // TILE):
        project(2 * group)
        project(2 * group + 1)
        rows = decode(
            jnp.concatenate([block_rows(packed_ref, 4 * group + n, parity) for n in range(4)], axis=0)
        )
        query = (silu(dot(rows, w_in_ref[:, 1024:1280])).astype(BF) * 0.0625).astype(BF)
        for head in range(HEADS):
            both = query[:, (head // 2) * 2 * DQK : (head // 2 + 1) * 2 * DQK]
            mine = (lane >= DQK) if head % 2 else (lane < DQK)
            query_scr[head] = jnp.where(mine, both, jnp.zeros_like(both))
        total_scr[...] = jnp.zeros_like(total_scr)
        base = group * 2 * TILE
        for start in range(0, base, TILE):
            tile(0, TILE, start, TILE)
        for pair in range(2):
            top = pair * 2 * TOK
            first = base + 2 * top
            if pair:
                tile(top, 2 * TOK, base, TILE)
            tile(top, 2 * TOK, first, 2 * TOK, (0, 0))
            tile(top + TOK, TOK, first + 2 * TOK, 2 * TOK, (2 * TOK, 1))

        attended = total_scr[...]
        centered = attended - jnp.mean(attended, axis=-1, keepdims=True)
        variance = jnp.mean(centered * centered, axis=-1, keepdims=True)
        normed = centered * lax.rsqrt(variance + norm_eps)
        gate_units = silu(dot(rows, w_in_ref[:, 0:512]))
        mixed_rows = (normed * gate_units).astype(BF)
        updated = rows.astype(F32) + dot(mixed_rows, w_out_ref[...])
        scale = lax.rsqrt(jnp.sum(updated * updated, axis=-1, keepdims=True) + unit_eps)
        user_ref[group * TILE : (group + 1) * TILE, :] = (updated * scale).astype(BF)

    table_copy.wait()
    row_ids = lax.broadcasted_iota(jnp.int32, (32, TOK), 1).astype(F32)
    for owner in range(32):
        asked = jnp.broadcast_to(rows_ref[:, owner : owner + 1], (32, TOK))
        rows = dot((row_ids == asked).astype(BF), table_scr[rank_of(owner)])
        used = (asked >= 0.0).astype(F32)
        for slot in range(2):
            entry_scr[4, pl.ds(slot * 32 + owner, 16, stride=64), :] = used[
                slot * 16 : (slot + 1) * 16
            ]
            for part in range(4):
                entry_scr[part, pl.ds(slot * 32 + owner, 16, stride=64), :] = rows[
                    slot * 16 : (slot + 1) * 16, part * 128 : (part + 1) * 128
                ]
    slot_ids = lax.broadcasted_iota(jnp.int32, (64, TOK), 0)
    exchange_ref[...] = jnp.zeros_like(exchange_ref)
    for block in range(CHIPS):
        entries = jnp.concatenate(
            [entry_scr[part, block * 64 : (block + 1) * 64, :] for part in range(4)], axis=1
        ).astype(BF)
        scores = dot(entries, user_ref[block * TOK : (block + 1) * TOK, :], NT) * inverse_sharpness
        used = entry_scr[4, block * 64 : (block + 1) * 64, :] > 0.0
        exps = jnp.where(used, jnp.exp(scores), 0.0)
        exps_ref[block] = exps
        hits = jnp.zeros((64, TOK), F32)
        for entry in range(4):
            place = label_places(labels_ref, block, entry, chip)
            hits = hits + (slot_ids == place).astype(F32)
        hits_ref[block] = hits
        total = jnp.sum(exps, axis=0, keepdims=True)
        exchange_ref[:, block : block + 1, :] = jnp.broadcast_to(total[None], (CHIPS, 1, TOK))
        exchange_ref[block, 16:17, :] = jnp.sum(hits * scores, axis=0, keepdims=True)


def gradient_kernel(
    exps_ref, hits_ref, user_ref, exchange_ref, labels_ref, rows_ref,
    send_ref, loss_ref, grad_scr,
):
    chip = lax.axis_index("z")
    sums = jnp.sum(exchange_ref[...], axis=0)
    positives = jnp.zeros((CHIPS, TOK), F32)
    for entry in range(4):
        positives = positives + (labels_ref[:, entry * TOK : (entry + 1) * TOK] >= 0.0).astype(F32)
    divisor = jnp.maximum(positives, 1.0)
    totals = sums[0:16]
    own = lax.broadcasted_iota(jnp.int32, (CHIPS, TOK), 0) == chip
    losses = (positives * jnp.log(totals) - sums[16:17]) / divisor
    loss_ref[...] = jnp.sum(jnp.where(own, losses, 0.0), axis=0, keepdims=True)
    exp_scale = positives / (divisor * totals)
    hit_scale = 1.0 / divisor
    for block in range(CHIPS):
        score_grad = (
            exps_ref[block] * exp_scale[block : block + 1]
            - hits_ref[block] * hit_scale[block : block + 1]
        ).astype(BF)
        grads = dot(score_grad, user_ref[block * TOK : (block + 1) * TOK, :]) * inverse_sharpness
        for slot in range(2):
            for part in range(4):
                for side in range(2):
                    at = side * SEND_ROWS + part * 32 + slot * 16 + block
                    first = slot * 32 + side * 16
                    grad_scr[pl.ds(at, 16, stride=2 * SEND_ROWS), :] = grads[
                        first : first + 16, part * 128 : (part + 1) * 128
                    ]
    sender = lax.axis_index("item") * 2 + lax.axis_index("core")
    at = lax.broadcasted_iota(jnp.int32, (32, TOK), 0) + (sender & 3) * 32
    spread = (lax.broadcasted_iota(jnp.int32, (32, TOK), 1) == at).astype(BF)
    index = dot(rows_ref[...].astype(BF), spread, (((0,), (0,)), ((), ())))[0:32]
    zeros = jnp.zeros((16, TOK), F32)
    for side in range(2):
        for extra in range(SEND_ROWS - TOK):
            rows = zeros if extra else index[side * 16 : (side + 1) * 16]
            grad_scr[pl.ds(side * SEND_ROWS + TOK + extra, 16, stride=2 * SEND_ROWS), :] = rows
    send_ref[...] = grad_scr[...].astype(BF)


def owner_kernel(
    arrived_ref, hidden_in_hbm, raw_hbm, w_in_hbm, w_out_hbm, gradient_ref,
    rows_scr, hidden_in_ref, raw_ref, w_in_ref, w_out_ref, sems,
):
    pairs = (
        (raw_hbm, raw_ref), (w_out_hbm, w_out_ref), (hidden_in_hbm, hidden_in_ref), (w_in_hbm, w_in_ref)
    )
    copies = [
        pltpu.make_async_copy(source, target, sems.at[n]) for n, (source, target) in enumerate(pairs)
    ]
    for copy in copies:
        copy.start()
    row_ids = lax.broadcasted_iota(jnp.int32, (TOK, TOK), 0).astype(F32)
    row_grad = jnp.zeros((TOK, WIDTH), F32)
    for group in range(8):
        extras = jnp.zeros((16, TOK), F32)
        for member in range(4):
            sender = group * 4 + member
            extras = extras + arrived_ref[sender, TOK:SEND_ROWS, :].astype(F32)
            for part in range(4):
                rows_scr[member * 32 : (member + 1) * 32, part * 128 : (part + 1) * 128] = arrived_ref[
                    sender, part * 32 : (part + 1) * 32, :
                ]
        index = extras[0:1]
        pick = (row_ids == index).astype(BF)
        row_grad = row_grad + dot(pick, rows_scr[...])
    for copy in copies:
        copy.wait()
    raw = raw_ref[...]
    inv_norm = lax.rsqrt(jnp.sum(raw * raw, axis=-1, keepdims=True) + unit_eps)
    unit = raw * inv_norm
    raw_grad = (row_grad - unit * jnp.sum(unit * row_grad, axis=-1, keepdims=True)) * inv_norm
    hidden_grad = split_product(raw_grad, w_out_ref[...])
    hidden_in = hidden_in_ref[...]
    sigma = 0.5 * jnp.tanh(0.5 * hidden_in) + 0.5
    input_grad = hidden_grad * (sigma * (1.0 + hidden_in * (1.0 - sigma)))
    gradient_ref[...] = split_product(input_grad, w_in_ref[...])


def on_device(
    history, w_in, w_out, item_table, w_item_in, w_item_out, req_rows, req_counts, labels
):
    with jax.named_scope("prepare"):
        packed, hidden_in, raw_embed, copies = call(
            prepare_kernel,
            (
                jax.ShapeDtypeStruct((PACK_ROWS, 128), jnp.int16),
                jax.ShapeDtypeStruct((TOK, HIDDEN), F32),
                jax.ShapeDtypeStruct((TOK, WIDTH), F32),
                jax.ShapeDtypeStruct((32, TOK, WIDTH), BF),
            ),
            "vvvvvvv",
        )(
            history[0], req_rows[0, 0].T, req_counts[0], labels[0].T,
            item_table, w_item_in, w_item_out,
        )

    with jax.named_scope("table_copies"):
        table = lax.all_to_all(copies, ("item", "core"), split_axis=0, concat_axis=0, tiled=True)

    with jax.named_scope("history_gather"):
        gathered = lax.all_gather(packed, ("z", "core"), axis=0, tiled=True)

    with jax.named_scope("tower"):
        user_rows, exps, hits, exchange, asked_rows, label_rows = call(
            tower_kernel,
            (
                jax.ShapeDtypeStruct((HALF, WIDTH), BF),
                jax.ShapeDtypeStruct((CHIPS, 64, TOK), F32),
                jax.ShapeDtypeStruct((CHIPS, 64, TOK), F32),
                jax.ShapeDtypeStruct((CHIPS, 24, TOK), F32),
                jax.ShapeDtypeStruct((32, TOK), F32),
                jax.ShapeDtypeStruct((CHIPS, WIDTH), F32),
            ),
            "vvvh",
            [
                pltpu.VMEM((HEADS * DQK, 2 * HALF), BF),
                pltpu.VMEM((2 * HALF, WIDTH), BF),
                pltpu.VMEM((HEADS, TILE, 2 * DQK), BF),
                pltpu.VMEM((TILE, WIDTH), F32),
                pltpu.VMEM((5, 1024, 128), F32),
                pltpu.VMEM((32, TOK, WIDTH), BF),
                pltpu.SemaphoreType.DMA,
            ],
        )(gathered.reshape(CHIPS, 2, PACK_ROWS, 128), w_in, w_out, table)

    with jax.named_scope("totals_exchange"):
        exchange = lax.all_to_all(exchange, "z", split_axis=0, concat_axis=0, tiled=True)

    with jax.named_scope("gradient_rows"):
        send, loss = call(
            gradient_kernel,
            (
                jax.ShapeDtypeStruct((32 * SEND_ROWS, 128), BF),
                jax.ShapeDtypeStruct((1, TOK), F32),
            ),
            "vvvvvv",
            [pltpu.VMEM((32 * SEND_ROWS, 128), F32)],
        )(exps, hits, user_rows, exchange, label_rows, asked_rows)

    with jax.named_scope("gradient_send"):
        arrived = lax.all_to_all(
            send.reshape(32, SEND_ROWS, 128), ("item", "core"), split_axis=0, concat_axis=0, tiled=True
        )

    with jax.named_scope("owner"):
        gradient = call(
            owner_kernel,
            jax.ShapeDtypeStruct((TOK, WIDTH), F32),
            "vhhhh",
            [
                pltpu.VMEM((TOK, WIDTH), BF),
                pltpu.VMEM((TOK, HIDDEN), F32),
                pltpu.VMEM((TOK, WIDTH), F32),
                pltpu.VMEM((WIDTH, HIDDEN), BF),
                pltpu.VMEM((HIDDEN, WIDTH), BF),
                pltpu.SemaphoreType.DMA((4,)),
            ],
        )(arrived, hidden_in, raw_embed, w_item_in, w_item_out)
    return (loss, gradient)


def solution(mesh):
    split = Mesh(mesh.devices.reshape(CHIPS, 2, 16), ("z", "core", "item"))
    rows = ("z", "core")
    placed = (
        P("item", rows, None),
        P(),
        P(),
        P(("z", "core", "item"), None),
        P(),
        P(),
        P("item", rows, None, None),
        P("item", rows, None),
        P("item", rows, None),
    )
    return jax.shard_map(
        on_device,
        mesh=split,
        in_specs=placed,
        out_specs=(P("item", rows), P(("z", "core", "item"), None)),
        check_vma=False,
    )
```

```python
import jax
import jax.numpy as jnp
from jax import lax
from jax.experimental import pallas as pl
from jax.experimental.pallas import tpu as pltpu
from jax.sharding import Mesh
from jax.sharding import PartitionSpec as P

HEADS = 4
DQK = 64
TOK = 128
WIDTH = 512
HIDDEN = 1024
CHIPS = 16
HALF = CHIPS * TOK
TILE = 512
PACK_ROWS = 528
SEND_ROWS = 136
RANGE = 6.0
CODES = 32760.0

inverse_sharpness = 50.0
norm_eps = 1e-05
unit_eps = 1e-06

BF = jnp.bfloat16
F32 = jnp.float32
VMEM_LIMIT = 24 * 1024 * 1024

NN = (((1,), (0,)), ((), ()))
NT = (((1,), (1,)), ((), ()))


def dot(left, right, contract=NN):
    return lax.dot_general(left, right, contract, preferred_element_type=F32)


def half_silu(half):
    return half + half * jnp.tanh(half)


def silu(inputs):
    return half_silu(0.5 * inputs)


def split_product(left, weight):
    high = left.astype(BF)
    low = (left - high.astype(F32)).astype(BF)
    return dot(high, weight, NT) + dot(low, weight, NT)


def call(kernel, out_shape, inputs, scratch=(), limit=VMEM_LIMIT):
    return pl.pallas_call(
        kernel,
        out_shape=out_shape,
        in_specs=[pl.BlockSpec(memory_space=pltpu.VMEM)] * inputs,
        out_specs=jax.tree.map(lambda _: pl.BlockSpec(memory_space=pltpu.VMEM), out_shape),
        scratch_shapes=list(scratch),
        compiler_params=pltpu.CompilerParams(vmem_limit_bytes=limit),
    )


def prepare_kernel(
    history_ref, wanted_ref, counts_ref, labels_ref, table_ref, w_in_ref, w_out_ref,
    packed_ref, hidden_in_ref, raw_ref, copies_ref,
):
    rows = history_ref[...].astype(F32)
    root = jnp.exp(jnp.log(jnp.abs(rows) * (1.0 / RANGE)) * (1.0 / 3.0)) * CODES
    codes = jnp.where(rows < 0.0, -root, root)
    codes = jnp.round(codes).astype(jnp.int32).astype(jnp.int16)
    for part in range(4):
        packed_ref[part * TOK : (part + 1) * TOK, :] = codes[:, part * 128 : (part + 1) * 128]
    wanted = wanted_ref[...]
    slot = lax.broadcasted_iota(jnp.int32, (2, WIDTH), 0)
    wanted = jnp.where(slot < counts_ref[...], wanted, -1)
    extras = [
        wanted[slot : slot + 1, part * 128 : (part + 1) * 128] for slot in range(2) for part in range(4)
    ]
    extras += [labels_ref[...], jnp.zeros((4, TOK), jnp.int32)]
    packed_ref[WIDTH:PACK_ROWS, :] = jnp.concatenate(extras, axis=0).astype(jnp.int16)

    hidden_in = dot(table_ref[...], w_in_ref[...])
    hidden_in_ref[...] = hidden_in
    raw = dot(silu(hidden_in).astype(BF), w_out_ref[...])
    raw_ref[...] = raw
    inv_norm = lax.rsqrt(jnp.sum(raw * raw, axis=-1, keepdims=True) + unit_eps)
    embedding = (raw * inv_norm).astype(BF)
    for rank in range(32):
        copies_ref[rank] = embedding


def decode(codes):
    root = codes.astype(F32) * (RANGE ** (1.0 / 3.0) / CODES)
    return (root * root * root).astype(BF)


def rank_of(owner):
    return (owner % 16) * 2 + owner // 16


def label_places(labels_ref, block, entry, chip):
    label = labels_ref[block : block + 1, entry * TOK : (entry + 1) * TOK].astype(jnp.int32)
    local = label - chip * 64
    inside = (label >= 0) & (local >= 0) & (local < 64)
    return jnp.where(inside, (local & 1) * 32 + (local >> 1), -1)


def block_rows(packed_ref, chip, core):
    parts = [packed_ref[chip, core, part * TOK : (part + 1) * TOK, :] for part in range(4)]
    return jnp.concatenate(parts, axis=1)


def tower_kernel(
    packed_ref, w_in_ref, w_out_ref, user_ref, rows_ref, labels_ref,
    key_scr, value_scr, query_scr, total_scr,
):
    parity = lax.axis_index("core")
    chip = lax.axis_index("z")

    shift = TOK - lax.rem(chip, 4) * 32
    row_at = lax.broadcasted_iota(jnp.int32, (16, TOK), 0)
    chip_row = lax.div(chip, 4)
    for block in range(CHIPS):
        extras = packed_ref[block, parity, WIDTH:PACK_ROWS, :].astype(F32)
        mine = pltpu.roll(extras, shift, 1)
        for slot in range(2):
            chosen = jnp.where(row_at == chip_row + 4 * slot, mine, 0.0)
            at = slot * CHIPS + block
            rows_ref[at : at + 1, :] = jnp.sum(chosen, axis=0, keepdims=True)
        labels_ref[block : block + 1, :] = jnp.concatenate(
            [extras[8 + entry : 9 + entry] for entry in range(4)], axis=1
        )

    def project(step):
        pieces = [block_rows(packed_ref, 2 * step + n // 2, n % 2) for n in range(4)]
        rows = decode(jnp.concatenate(pieces, axis=0))
        at = slice(step * TILE, (step + 1) * TILE)
        value_scr[at, :] = silu(dot(rows, w_in_ref[:, 512:1024])).astype(BF)
        key_scr[:, at] = silu(dot(w_in_ref[:, 1280:1536], rows, (((0,), (1,)), ((), ())))).astype(BF)

    lane = lax.broadcasted_iota(jnp.int32, (TILE, 2 * DQK), 1)

    def tile(top, height, start, width, diagonal=None):
        if diagonal is not None:
            row = lax.broadcasted_iota(jnp.int32, (height, width), 0)
            key_at = lax.broadcasted_iota(jnp.int32, (height, width), 1) + diagonal[0]
            block = row // TOK + diagonal[1]
            allowed = key_at <= (2 * block + parity) * TOK + row % TOK
        weights = []
        for head in range(HEADS):
            keys = key_scr[(head // 2) * 2 * DQK : (head // 2 + 1) * 2 * DQK, start : start + width]
            weight = half_silu(dot(query_scr[head, top : top + height], keys))
            if diagonal is not None:
                weight = jnp.where(allowed, weight, 0.0)
            weights.append(weight.astype(BF))
        for head in range(HEADS):
            values = value_scr[start : start + width, head * 128 : (head + 1) * 128]
            total_scr[top : top + height, head * 128 : (head + 1) * 128] += dot(weights[head], values)

    for group in range(HALF // TILE):
        project(2 * group)
        project(2 * group + 1)
        rows = decode(
            jnp.concatenate([block_rows(packed_ref, 4 * group + n, parity) for n in range(4)], axis=0)
        )
        query = (silu(dot(rows, w_in_ref[:, 1024:1280])).astype(BF) * 0.0625).astype(BF)
        for head in range(HEADS):
            both = query[:, (head // 2) * 2 * DQK : (head // 2 + 1) * 2 * DQK]
            mine = (lane >= DQK) if head % 2 else (lane < DQK)
            query_scr[head] = jnp.where(mine, both, jnp.zeros_like(both))
        total_scr[...] = jnp.zeros_like(total_scr)
        base = group * 2 * TILE
        for start in range(0, base, TILE):
            tile(0, TILE, start, TILE)
        for pair in range(2):
            top = pair * 2 * TOK
            first = base + 2 * top
            if pair:
                tile(top, 2 * TOK, base, TILE)
            tile(top, 2 * TOK, first, 2 * TOK, (0, 0))
            tile(top + TOK, TOK, first + 2 * TOK, 2 * TOK, (2 * TOK, 1))

        attended = total_scr[...]
        centered = attended - jnp.mean(attended, axis=-1, keepdims=True)
        variance = jnp.mean(centered * centered, axis=-1, keepdims=True)
        normed = centered * lax.rsqrt(variance + norm_eps)
        gate_units = silu(dot(rows, w_in_ref[:, 0:512]))
        mixed_rows = (normed * gate_units).astype(BF)
        updated = rows.astype(F32) + dot(mixed_rows, w_out_ref[...])
        scale = lax.rsqrt(jnp.sum(updated * updated, axis=-1, keepdims=True) + unit_eps)
        user_ref[group * TILE : (group + 1) * TILE, :] = (updated * scale).astype(BF)


def scores_kernel(
    table_ref, user_ref, rows_ref, labels_ref, exps_ref, hits_ref, exchange_ref, entry_scr
):
    chip = lax.axis_index("z")
    row_ids = lax.broadcasted_iota(jnp.int32, (32, TOK), 1).astype(F32)
    for owner in range(32):
        asked = jnp.broadcast_to(rows_ref[:, owner : owner + 1], (32, TOK))
        rows = dot((row_ids == asked).astype(BF), table_ref[rank_of(owner)])
        used = (asked >= 0.0).astype(F32)
        for slot in range(2):
            entry_scr[4, pl.ds(slot * 32 + owner, 16, stride=64), :] = used[
                slot * 16 : (slot + 1) * 16
            ]
            for part in range(4):
                entry_scr[part, pl.ds(slot * 32 + owner, 16, stride=64), :] = rows[
                    slot * 16 : (slot + 1) * 16, part * 128 : (part + 1) * 128
                ]
    slot_ids = lax.broadcasted_iota(jnp.int32, (64, TOK), 0)
    exchange_ref[...] = jnp.zeros_like(exchange_ref)
    for block in range(CHIPS):
        entries = jnp.concatenate(
            [entry_scr[part, block * 64 : (block + 1) * 64, :] for part in range(4)], axis=1
        ).astype(BF)
        scores = dot(entries, user_ref[block * TOK : (block + 1) * TOK, :], NT) * inverse_sharpness
        used = entry_scr[4, block * 64 : (block + 1) * 64, :] > 0.0
        exps = jnp.where(used, jnp.exp(scores), 0.0)
        exps_ref[block] = exps
        hits = jnp.zeros((64, TOK), F32)
        for entry in range(4):
            place = label_places(labels_ref, block, entry, chip)
            hits = hits + (slot_ids == place).astype(F32)
        hits_ref[block] = hits
        total = jnp.sum(exps, axis=0, keepdims=True)
        exchange_ref[:, block : block + 1, :] = jnp.broadcast_to(total[None], (CHIPS, 1, TOK))
        exchange_ref[block, 16:17, :] = jnp.sum(hits * scores, axis=0, keepdims=True)


def gradient_kernel(
    exps_ref, hits_ref, user_ref, exchange_ref, labels_ref, rows_ref,
    send_ref, loss_ref, grad_scr,
):
    chip = lax.axis_index("z")
    sums = jnp.sum(exchange_ref[...], axis=0)
    positives = jnp.zeros((CHIPS, TOK), F32)
    for entry in range(4):
        positives = positives + (labels_ref[:, entry * TOK : (entry + 1) * TOK] >= 0.0).astype(F32)
    divisor = jnp.maximum(positives, 1.0)
    totals = sums[0:16]
    own = lax.broadcasted_iota(jnp.int32, (CHIPS, TOK), 0) == chip
    losses = (positives * jnp.log(totals) - sums[16:17]) / divisor
    loss_ref[...] = jnp.sum(jnp.where(own, losses, 0.0), axis=0, keepdims=True)
    exp_scale = positives / (divisor * totals)
    hit_scale = 1.0 / divisor
    for block in range(CHIPS):
        score_grad = (
            exps_ref[block] * exp_scale[block : block + 1]
            - hits_ref[block] * hit_scale[block : block + 1]
        ).astype(BF)
        grads = dot(score_grad, user_ref[block * TOK : (block + 1) * TOK, :]) * inverse_sharpness
        for slot in range(2):
            for part in range(4):
                for side in range(2):
                    at = side * SEND_ROWS + part * 32 + slot * 16 + block
                    first = slot * 32 + side * 16
                    grad_scr[pl.ds(at, 16, stride=2 * SEND_ROWS), :] = grads[
                        first : first + 16, part * 128 : (part + 1) * 128
                    ]
    sender = lax.axis_index("item") * 2 + lax.axis_index("core")
    at = lax.broadcasted_iota(jnp.int32, (32, TOK), 0) + (sender & 3) * 32
    spread = (lax.broadcasted_iota(jnp.int32, (32, TOK), 1) == at).astype(BF)
    index = dot(rows_ref[...].astype(BF), spread, (((0,), (0,)), ((), ())))[0:32]
    zeros = jnp.zeros((16, TOK), F32)
    for side in range(2):
        for extra in range(SEND_ROWS - TOK):
            rows = zeros if extra else index[side * 16 : (side + 1) * 16]
            grad_scr[pl.ds(side * SEND_ROWS + TOK + extra, 16, stride=2 * SEND_ROWS), :] = rows
    send_ref[...] = grad_scr[...].astype(BF)


def owner_kernel(
    arrived_ref, index_ref, hidden_in_ref, raw_ref, w_in_ref, w_out_ref, gradient_ref, rows_scr
):
    row_ids = lax.broadcasted_iota(jnp.int32, (TOK, TOK), 0).astype(F32)
    row_grad = jnp.zeros((TOK, WIDTH), F32)
    for group in range(8):
        index = jnp.zeros((1, TOK), F32)
        for member in range(4):
            sender = group * 4 + member
            index = index + index_ref[sender : sender + 1, :]
            for part in range(4):
                rows_scr[member * 32 : (member + 1) * 32, part * 128 : (part + 1) * 128] = arrived_ref[
                    sender, part * 32 : (part + 1) * 32, :
                ]
        pick = (row_ids == index).astype(BF)
        row_grad = row_grad + dot(pick, rows_scr[...])
    raw = raw_ref[...]
    inv_norm = lax.rsqrt(jnp.sum(raw * raw, axis=-1, keepdims=True) + unit_eps)
    unit = raw * inv_norm
    raw_grad = (row_grad - unit * jnp.sum(unit * row_grad, axis=-1, keepdims=True)) * inv_norm
    hidden_grad = split_product(raw_grad, w_out_ref[...])
    hidden_in = hidden_in_ref[...]
    sigma = 0.5 * jnp.tanh(0.5 * hidden_in) + 0.5
    input_grad = hidden_grad * (sigma * (1.0 + hidden_in * (1.0 - sigma)))
    gradient_ref[...] = split_product(input_grad, w_in_ref[...])


def on_device(
    history, w_in, w_out, item_table, w_item_in, w_item_out, req_rows, req_counts, labels
):
    with jax.named_scope("prepare"):
        packed, hidden_in, raw_embed, copies = call(
            prepare_kernel,
            (
                jax.ShapeDtypeStruct((PACK_ROWS, 128), jnp.int16),
                jax.ShapeDtypeStruct((TOK, HIDDEN), F32),
                jax.ShapeDtypeStruct((TOK, WIDTH), F32),
                jax.ShapeDtypeStruct((32, TOK, WIDTH), BF),
            ),
            7,
        )(
            history[0], req_rows[0, 0].T, req_counts[0], labels[0].T,
            item_table, w_item_in, w_item_out,
        )

    with jax.named_scope("table_copies"):
        table = lax.all_to_all(copies, ("item", "core"), split_axis=0, concat_axis=0, tiled=True)

    with jax.named_scope("history_gather"):
        gathered = lax.all_gather(packed, ("z", "core"), axis=0, tiled=True)

    with jax.named_scope("tower"):
        user_rows, asked_rows, label_rows = call(
            tower_kernel,
            (
                jax.ShapeDtypeStruct((HALF, WIDTH), BF),
                jax.ShapeDtypeStruct((32, TOK), F32),
                jax.ShapeDtypeStruct((CHIPS, WIDTH), F32),
            ),
            3,
            [
                pltpu.VMEM((HEADS * DQK, 2 * HALF), BF),
                pltpu.VMEM((2 * HALF, WIDTH), BF),
                pltpu.VMEM((HEADS, TILE, 2 * DQK), BF),
                pltpu.VMEM((TILE, WIDTH), F32),
            ],
        )(gathered.reshape(CHIPS, 2, PACK_ROWS, 128), w_in, w_out)

    with jax.named_scope("scores"):
        exps, hits, exchange = call(
            scores_kernel,
            (
                jax.ShapeDtypeStruct((CHIPS, 64, TOK), F32),
                jax.ShapeDtypeStruct((CHIPS, 64, TOK), F32),
                jax.ShapeDtypeStruct((CHIPS, 24, TOK), F32),
            ),
            4,
            [pltpu.VMEM((5, 1024, 128), F32)],
        )(table, user_rows, asked_rows, label_rows)

    with jax.named_scope("totals_exchange"):
        exchange = lax.all_to_all(exchange, "z", split_axis=0, concat_axis=0, tiled=True)

    with jax.named_scope("gradient_rows"):
        send, loss = call(
            gradient_kernel,
            (
                jax.ShapeDtypeStruct((32 * SEND_ROWS, 128), BF),
                jax.ShapeDtypeStruct((1, TOK), F32),
            ),
            6,
            [pltpu.VMEM((32 * SEND_ROWS, 128), F32)],
        )(exps, hits, user_rows, exchange, label_rows, asked_rows)

    with jax.named_scope("gradient_send"):
        arrived = lax.all_to_all(
            send.reshape(32, SEND_ROWS, 128), ("item", "core"), split_axis=0, concat_axis=0, tiled=True
        )

    with jax.named_scope("owner"):
        gradient = call(
            owner_kernel,
            jax.ShapeDtypeStruct((TOK, WIDTH), F32),
            6,
            [pltpu.VMEM((TOK, WIDTH), BF)],
        )(arrived, arrived[:, TOK].astype(F32), hidden_in, raw_embed, w_item_in, w_item_out)
    return (loss, gradient)


def solution(mesh):
    split = Mesh(mesh.devices.reshape(CHIPS, 2, 16), ("z", "core", "item"))
    rows = ("z", "core")
    placed = (
        P("item", rows, None),
        P(),
        P(),
        P(("z", "core", "item"), None),
        P(),
        P(),
        P("item", rows, None, None),
        P("item", rows, None),
        P("item", rows, None),
    )
    return jax.shard_map(
        on_device,
        mesh=split,
        in_specs=placed,
        out_specs=(P("item", rows), P(("z", "core", "item"), None)),
        check_vma=False,
    )
```

```python
import jax
import jax.numpy as jnp
from jax import lax
from jax.experimental import pallas as pl
from jax.experimental.pallas import tpu as pltpu
from jax.sharding import Mesh
from jax.sharding import PartitionSpec as P

HEADS = 4
DQK = 64
TOK = 128
WIDTH = 512
HIDDEN = 1024
CHIPS = 16
HALF = CHIPS * TOK
TILE = 512
PACK_ROWS = 528
SEND_ROWS = 136
RANGE = 6.0
CODES = 32760.0

inverse_sharpness = 50.0
norm_eps = 1e-05
unit_eps = 1e-06

BF = jnp.bfloat16
F32 = jnp.float32
VMEM_LIMIT = 24 * 1024 * 1024
LARGE_LIMIT = 56 * 1024 * 1024

NN = (((1,), (0,)), ((), ()))
NT = (((1,), (1,)), ((), ()))


def dot(left, right, contract=NN):
    return lax.dot_general(left, right, contract, preferred_element_type=F32)


def half_silu(half):
    return half + half * jnp.tanh(half)


def silu(inputs):
    return half_silu(0.5 * inputs)


def split_product(left, weight):
    high = left.astype(BF)
    low = (left - high.astype(F32)).astype(BF)
    return dot(high, weight, NT) + dot(low, weight, NT)


def call(kernel, out_shape, inputs, scratch=(), limit=VMEM_LIMIT):
    return pl.pallas_call(
        kernel,
        out_shape=out_shape,
        in_specs=[pl.BlockSpec(memory_space=pltpu.VMEM)] * inputs,
        out_specs=jax.tree.map(lambda _: pl.BlockSpec(memory_space=pltpu.VMEM), out_shape),
        scratch_shapes=list(scratch),
        compiler_params=pltpu.CompilerParams(vmem_limit_bytes=limit),
    )


def prepare_kernel(
    history_ref, wanted_ref, counts_ref, labels_ref, table_ref, w_in_ref, w_out_ref,
    packed_ref, hidden_in_ref, raw_ref, copies_ref,
):
    rows = history_ref[...].astype(F32)
    root = jnp.exp(jnp.log(jnp.abs(rows) * (1.0 / RANGE)) * (1.0 / 3.0)) * CODES
    codes = jnp.where(rows < 0.0, -root, root)
    codes = jnp.round(codes).astype(jnp.int32).astype(jnp.int16)
    for part in range(4):
        packed_ref[part * TOK : (part + 1) * TOK, :] = codes[:, part * 128 : (part + 1) * 128]
    wanted = wanted_ref[...]
    slot = lax.broadcasted_iota(jnp.int32, (2, WIDTH), 0)
    wanted = jnp.where(slot < counts_ref[...], wanted, -1)
    extras = [
        wanted[slot : slot + 1, part * 128 : (part + 1) * 128] for slot in range(2) for part in range(4)
    ]
    extras += [labels_ref[...], jnp.zeros((4, TOK), jnp.int32)]
    packed_ref[WIDTH:PACK_ROWS, :] = jnp.concatenate(extras, axis=0).astype(jnp.int16)

    hidden_in = dot(table_ref[...], w_in_ref[...])
    hidden_in_ref[...] = hidden_in
    raw = dot(silu(hidden_in).astype(BF), w_out_ref[...])
    raw_ref[...] = raw
    inv_norm = lax.rsqrt(jnp.sum(raw * raw, axis=-1, keepdims=True) + unit_eps)
    embedding = (raw * inv_norm).astype(BF)
    for rank in range(32):
        copies_ref[rank] = embedding


def decode(codes):
    root = codes.astype(F32) * (RANGE ** (1.0 / 3.0) / CODES)
    return (root * root * root).astype(BF)


def rank_of(owner):
    return (owner % 16) * 2 + owner // 16


def label_places(labels_ref, block, entry, chip):
    label = labels_ref[block : block + 1, entry * TOK : (entry + 1) * TOK].astype(jnp.int32)
    local = label - chip * 64
    inside = (label >= 0) & (local >= 0) & (local < 64)
    return jnp.where(inside, (local & 1) * 32 + (local >> 1), -1)


def block_rows(packed_ref, chip, core):
    parts = [packed_ref[chip, core, part * TOK : (part + 1) * TOK, :] for part in range(4)]
    return jnp.concatenate(parts, axis=1)


def tower_kernel(
    packed_ref, w_in_ref, w_out_ref, user_ref, rows_ref, labels_ref,
    key_scr, value_scr, query_scr, total_scr,
):
    parity = lax.axis_index("core")
    chip = lax.axis_index("z")

    shift = TOK - lax.rem(chip, 4) * 32
    row_at = lax.broadcasted_iota(jnp.int32, (16, TOK), 0)
    chip_row = lax.div(chip, 4)
    for block in range(CHIPS):
        extras = packed_ref[block, parity, WIDTH:PACK_ROWS, :].astype(F32)
        mine = pltpu.roll(extras, shift, 1)
        for slot in range(2):
            chosen = jnp.where(row_at == chip_row + 4 * slot, mine, 0.0)
            at = slot * CHIPS + block
            rows_ref[at : at + 1, :] = jnp.sum(chosen, axis=0, keepdims=True)
        labels_ref[block : block + 1, :] = jnp.concatenate(
            [extras[8 + entry : 9 + entry] for entry in range(4)], axis=1
        )

    def project(step, carry):
        pieces = [block_rows(packed_ref, 2 * step + n // 2, n % 2) for n in range(4)]
        rows = decode(jnp.concatenate(pieces, axis=0))
        at = pl.ds(pl.multiple_of(step * TILE, TILE), TILE)
        value_scr[at, :] = silu(dot(rows, w_in_ref[:, 512:1024])).astype(BF)
        key_scr[:, at] = silu(dot(w_in_ref[:, 1280:1536], rows, (((0,), (1,)), ((), ())))).astype(BF)
        return carry

    lax.fori_loop(0, 2 * HALF // TILE, project, 0)

    lane = lax.broadcasted_iota(jnp.int32, (TILE, 2 * DQK), 1)

    def tile(top, height, start, width, diagonal=None):
        if diagonal is not None:
            row = lax.broadcasted_iota(jnp.int32, (height, width), 0)
            key_at = lax.broadcasted_iota(jnp.int32, (height, width), 1) + diagonal[0]
            block = row // TOK + diagonal[1]
            allowed = key_at <= (2 * block + parity) * TOK + row % TOK
        weights = []
        for head in range(HEADS):
            keys = key_scr[(head // 2) * 2 * DQK : (head // 2 + 1) * 2 * DQK, pl.ds(start, width)]
            weight = half_silu(dot(query_scr[head, top : top + height], keys))
            if diagonal is not None:
                weight = jnp.where(allowed, weight, 0.0)
            weights.append(weight.astype(BF))
        for head in range(HEADS):
            values = value_scr[pl.ds(start, width), head * 128 : (head + 1) * 128]
            total_scr[top : top + height, head * 128 : (head + 1) * 128] += dot(weights[head], values)

    for group in range(HALF // TILE):
        rows = decode(
            jnp.concatenate([block_rows(packed_ref, 4 * group + n, parity) for n in range(4)], axis=0)
        )
        query = (silu(dot(rows, w_in_ref[:, 1024:1280])).astype(BF) * 0.0625).astype(BF)
        for head in range(HEADS):
            both = query[:, (head // 2) * 2 * DQK : (head // 2 + 1) * 2 * DQK]
            mine = (lane >= DQK) if head % 2 else (lane < DQK)
            query_scr[head] = jnp.where(mine, both, jnp.zeros_like(both))
        total_scr[...] = jnp.zeros_like(total_scr)
        base = group * 2 * TILE

        def earlier(step, carry):
            tile(0, TILE, pl.multiple_of(step * TILE, TILE), TILE)
            return carry

        lax.fori_loop(0, base // TILE, earlier, 0)
        for pair in range(2):
            top = pair * 2 * TOK
            first = base + 2 * top
            if pair:
                tile(top, 2 * TOK, base, TILE)
            tile(top, 2 * TOK, first, 2 * TOK, (0, 0))
            tile(top + TOK, TOK, first + 2 * TOK, 2 * TOK, (2 * TOK, 1))

        attended = total_scr[...]
        centered = attended - jnp.mean(attended, axis=-1, keepdims=True)
        variance = jnp.mean(centered * centered, axis=-1, keepdims=True)
        normed = centered * lax.rsqrt(variance + norm_eps)
        gate_units = silu(dot(rows, w_in_ref[:, 0:512]))
        mixed_rows = (normed * gate_units).astype(BF)
        updated = rows.astype(F32) + dot(mixed_rows, w_out_ref[...])
        scale = lax.rsqrt(jnp.sum(updated * updated, axis=-1, keepdims=True) + unit_eps)
        user_ref[group * TILE : (group + 1) * TILE, :] = (updated * scale).astype(BF)


def scores_kernel(
    table_ref, user_ref, rows_ref, labels_ref, exps_ref, hits_ref, exchange_ref, entry_scr
):
    chip = lax.axis_index("z")
    row_ids = lax.broadcasted_iota(jnp.int32, (32, TOK), 1).astype(F32)
    for owner in range(32):
        asked = jnp.broadcast_to(rows_ref[:, owner : owner + 1], (32, TOK))
        rows = dot((row_ids == asked).astype(BF), table_ref[rank_of(owner)])
        used = (asked >= 0.0).astype(F32)
        for slot in range(2):
            entry_scr[4, pl.ds(slot * 32 + owner, 16, stride=64), :] = used[
                slot * 16 : (slot + 1) * 16
            ]
            for part in range(4):
                entry_scr[part, pl.ds(slot * 32 + owner, 16, stride=64), :] = rows[
                    slot * 16 : (slot + 1) * 16, part * 128 : (part + 1) * 128
                ]
    slot_ids = lax.broadcasted_iota(jnp.int32, (64, TOK), 0)
    exchange_ref[...] = jnp.zeros_like(exchange_ref)
    for block in range(CHIPS):
        entries = jnp.concatenate(
            [entry_scr[part, block * 64 : (block + 1) * 64, :] for part in range(4)], axis=1
        ).astype(BF)
        scores = dot(entries, user_ref[block * TOK : (block + 1) * TOK, :], NT) * inverse_sharpness
        used = entry_scr[4, block * 64 : (block + 1) * 64, :] > 0.0
        exps = jnp.where(used, jnp.exp(scores), 0.0)
        exps_ref[block] = exps
        hits = jnp.zeros((64, TOK), F32)
        for entry in range(4):
            place = label_places(labels_ref, block, entry, chip)
            hits = hits + (slot_ids == place).astype(F32)
        hits_ref[block] = hits
        total = jnp.sum(exps, axis=0, keepdims=True)
        exchange_ref[:, block : block + 1, :] = jnp.broadcast_to(total[None], (CHIPS, 1, TOK))
        exchange_ref[block, 16:17, :] = jnp.sum(hits * scores, axis=0, keepdims=True)


def gradient_kernel(
    exps_ref, hits_ref, user_ref, exchange_ref, labels_ref, rows_ref,
    send_ref, loss_ref, grad_scr,
):
    chip = lax.axis_index("z")
    sums = jnp.sum(exchange_ref[...], axis=0)
    positives = jnp.zeros((CHIPS, TOK), F32)
    for entry in range(4):
        positives = positives + (labels_ref[:, entry * TOK : (entry + 1) * TOK] >= 0.0).astype(F32)
    divisor = jnp.maximum(positives, 1.0)
    totals = sums[0:16]
    own = lax.broadcasted_iota(jnp.int32, (CHIPS, TOK), 0) == chip
    losses = (positives * jnp.log(totals) - sums[16:17]) / divisor
    loss_ref[...] = jnp.sum(jnp.where(own, losses, 0.0), axis=0, keepdims=True)
    exp_scale = positives / (divisor * totals)
    hit_scale = 1.0 / divisor
    for block in range(CHIPS):
        score_grad = (
            exps_ref[block] * exp_scale[block : block + 1]
            - hits_ref[block] * hit_scale[block : block + 1]
        ).astype(BF)
        grads = dot(score_grad, user_ref[block * TOK : (block + 1) * TOK, :]) * inverse_sharpness
        for slot in range(2):
            for part in range(4):
                for side in range(2):
                    at = side * SEND_ROWS + part * 32 + slot * 16 + block
                    first = slot * 32 + side * 16
                    grad_scr[pl.ds(at, 16, stride=2 * SEND_ROWS), :] = grads[
                        first : first + 16, part * 128 : (part + 1) * 128
                    ]
    sender = lax.axis_index("item") * 2 + lax.axis_index("core")
    at = lax.broadcasted_iota(jnp.int32, (32, TOK), 0) + (sender & 3) * 32
    spread = (lax.broadcasted_iota(jnp.int32, (32, TOK), 1) == at).astype(BF)
    index = dot(rows_ref[...].astype(BF), spread, (((0,), (0,)), ((), ())))[0:32]
    zeros = jnp.zeros((16, TOK), F32)
    for side in range(2):
        for extra in range(SEND_ROWS - TOK):
            rows = zeros if extra else index[side * 16 : (side + 1) * 16]
            grad_scr[pl.ds(side * SEND_ROWS + TOK + extra, 16, stride=2 * SEND_ROWS), :] = rows
    send_ref[...] = grad_scr[...].astype(BF)


def owner_kernel(
    arrived_ref, index_ref, hidden_in_ref, raw_ref, w_in_ref, w_out_ref, gradient_ref, rows_scr
):
    row_ids = lax.broadcasted_iota(jnp.int32, (TOK, TOK), 0).astype(F32)
    row_grad = jnp.zeros((TOK, WIDTH), F32)
    for group in range(8):
        index = jnp.zeros((1, TOK), F32)
        for member in range(4):
            sender = group * 4 + member
            index = index + index_ref[sender : sender + 1, :]
            for part in range(4):
                rows_scr[member * 32 : (member + 1) * 32, part * 128 : (part + 1) * 128] = arrived_ref[
                    sender, part * 32 : (part + 1) * 32, :
                ]
        pick = (row_ids == index).astype(BF)
        row_grad = row_grad + dot(pick, rows_scr[...])
    raw = raw_ref[...]
    inv_norm = lax.rsqrt(jnp.sum(raw * raw, axis=-1, keepdims=True) + unit_eps)
    unit = raw * inv_norm
    raw_grad = (row_grad - unit * jnp.sum(unit * row_grad, axis=-1, keepdims=True)) * inv_norm
    hidden_grad = split_product(raw_grad, w_out_ref[...])
    hidden_in = hidden_in_ref[...]
    sigma = 0.5 * jnp.tanh(0.5 * hidden_in) + 0.5
    input_grad = hidden_grad * (sigma * (1.0 + hidden_in * (1.0 - sigma)))
    gradient_ref[...] = split_product(input_grad, w_in_ref[...])


def on_device(
    history, w_in, w_out, item_table, w_item_in, w_item_out, req_rows, req_counts, labels
):
    with jax.named_scope("prepare"):
        packed, hidden_in, raw_embed, copies = call(
            prepare_kernel,
            (
                jax.ShapeDtypeStruct((PACK_ROWS, 128), jnp.int16),
                jax.ShapeDtypeStruct((TOK, HIDDEN), F32),
                jax.ShapeDtypeStruct((TOK, WIDTH), F32),
                jax.ShapeDtypeStruct((32, TOK, WIDTH), BF),
            ),
            7,
            limit=LARGE_LIMIT,
        )(
            history[0], req_rows[0, 0].T, req_counts[0], labels[0].T,
            item_table, w_item_in, w_item_out,
        )

    with jax.named_scope("table_copies"):
        table = lax.all_to_all(copies, ("item", "core"), split_axis=0, concat_axis=0, tiled=True)

    with jax.named_scope("history_gather"):
        gathered = lax.all_gather(packed, ("z", "core"), axis=0, tiled=True)

    with jax.named_scope("tower"):
        user_rows, asked_rows, label_rows = call(
            tower_kernel,
            (
                jax.ShapeDtypeStruct((HALF, WIDTH), BF),
                jax.ShapeDtypeStruct((32, TOK), F32),
                jax.ShapeDtypeStruct((CHIPS, WIDTH), F32),
            ),
            3,
            [
                pltpu.VMEM((HEADS * DQK, 2 * HALF), BF),
                pltpu.VMEM((2 * HALF, WIDTH), BF),
                pltpu.VMEM((HEADS, TILE, 2 * DQK), BF),
                pltpu.VMEM((TILE, WIDTH), F32),
            ],
        )(gathered.reshape(CHIPS, 2, PACK_ROWS, 128), w_in, w_out)

    with jax.named_scope("scores"):
        exps, hits, exchange = call(
            scores_kernel,
            (
                jax.ShapeDtypeStruct((CHIPS, 64, TOK), F32),
                jax.ShapeDtypeStruct((CHIPS, 64, TOK), F32),
                jax.ShapeDtypeStruct((CHIPS, 24, TOK), F32),
            ),
            4,
            [pltpu.VMEM((5, 1024, 128), F32)],
        )(table, user_rows, asked_rows, label_rows)

    with jax.named_scope("totals_exchange"):
        exchange = lax.all_to_all(exchange, "z", split_axis=0, concat_axis=0, tiled=True)

    with jax.named_scope("gradient_rows"):
        send, loss = call(
            gradient_kernel,
            (
                jax.ShapeDtypeStruct((32 * SEND_ROWS, 128), BF),
                jax.ShapeDtypeStruct((1, TOK), F32),
            ),
            6,
            [pltpu.VMEM((32 * SEND_ROWS, 128), F32)],
        )(exps, hits, user_rows, exchange, label_rows, asked_rows)

    with jax.named_scope("gradient_send"):
        arrived = lax.all_to_all(
            send.reshape(32, SEND_ROWS, 128), ("item", "core"), split_axis=0, concat_axis=0, tiled=True
        )

    with jax.named_scope("owner"):
        gradient = call(
            owner_kernel,
            jax.ShapeDtypeStruct((TOK, WIDTH), F32),
            6,
            [pltpu.VMEM((TOK, WIDTH), BF)],
        )(arrived, arrived[:, TOK].astype(F32), hidden_in, raw_embed, w_item_in, w_item_out)
    return (loss, gradient)


def solution(mesh):
    split = Mesh(mesh.devices.reshape(CHIPS, 2, 16), ("z", "core", "item"))
    rows = ("z", "core")
    placed = (
        P("item", rows, None),
        P(),
        P(),
        P(("z", "core", "item"), None),
        P(),
        P(),
        P("item", rows, None, None),
        P("item", rows, None),
        P("item", rows, None),
    )
    return jax.shard_map(
        on_device,
        mesh=split,
        in_specs=placed,
        out_specs=(P("item", rows), P(("z", "core", "item"), None)),
        check_vma=False,
    )
```

```python
import jax
import jax.numpy as jnp
from jax import lax
from jax.experimental import pallas as pl
from jax.experimental.pallas import tpu as pltpu
from jax.sharding import Mesh
from jax.sharding import PartitionSpec as P

HEADS = 4
DQK = 64
TOK = 128
WIDTH = 512
HIDDEN = 1024
CHIPS = 16
HALF = CHIPS * TOK
TILE = 512
PACK_ROWS = 528
SEND_ROWS = 136
RANGE = 6.0
CODES = 32760.0

inverse_sharpness = 50.0
norm_eps = 1e-05
unit_eps = 1e-06

BF = jnp.bfloat16
F32 = jnp.float32
VMEM_LIMIT = 24 * 1024 * 1024
LARGE_LIMIT = 56 * 1024 * 1024
TOWER_LIMIT = 32 * 1024 * 1024

NN = (((1,), (0,)), ((), ()))
NT = (((1,), (1,)), ((), ()))


def dot(left, right, contract=NN):
    return lax.dot_general(left, right, contract, preferred_element_type=F32)


def half_silu(half):
    return half + half * jnp.tanh(half)


def silu(inputs):
    return half_silu(0.5 * inputs)


def split_product(left, weight):
    high = left.astype(BF)
    low = (left - high.astype(F32)).astype(BF)
    return dot(high, weight, NT) + dot(low, weight, NT)


def call(kernel, out_shape, inputs, scratch=(), limit=VMEM_LIMIT):
    return pl.pallas_call(
        kernel,
        out_shape=out_shape,
        in_specs=[pl.BlockSpec(memory_space=pltpu.VMEM)] * inputs,
        out_specs=jax.tree.map(lambda _: pl.BlockSpec(memory_space=pltpu.VMEM), out_shape),
        scratch_shapes=list(scratch),
        compiler_params=pltpu.CompilerParams(vmem_limit_bytes=limit),
    )


def prepare_kernel(
    history_ref, wanted_ref, counts_ref, labels_ref, table_ref, w_in_ref, w_out_ref,
    packed_ref, hidden_in_ref, raw_ref, copies_ref,
):
    rows = history_ref[...].astype(F32)
    root = jnp.exp(jnp.log(jnp.abs(rows) * (1.0 / RANGE)) * (1.0 / 3.0)) * CODES
    codes = jnp.where(rows < 0.0, -root, root)
    codes = jnp.round(codes).astype(jnp.int32).astype(jnp.int16)
    for part in range(4):
        packed_ref[part * TOK : (part + 1) * TOK, :] = codes[:, part * 128 : (part + 1) * 128]
    wanted = wanted_ref[...]
    slot = lax.broadcasted_iota(jnp.int32, (2, WIDTH), 0)
    wanted = jnp.where(slot < counts_ref[...], wanted, -1)
    extras = [
        wanted[slot : slot + 1, part * 128 : (part + 1) * 128] for slot in range(2) for part in range(4)
    ]
    extras += [labels_ref[...], jnp.zeros((4, TOK), jnp.int32)]
    packed_ref[WIDTH:PACK_ROWS, :] = jnp.concatenate(extras, axis=0).astype(jnp.int16)

    hidden_in = dot(table_ref[...], w_in_ref[...])
    hidden_in_ref[...] = hidden_in
    raw = dot(silu(hidden_in).astype(BF), w_out_ref[...])
    raw_ref[...] = raw
    inv_norm = lax.rsqrt(jnp.sum(raw * raw, axis=-1, keepdims=True) + unit_eps)
    embedding = (raw * inv_norm).astype(BF)
    for rank in range(32):
        copies_ref[rank] = embedding


def decode(codes):
    root = codes.astype(F32) * (RANGE ** (1.0 / 3.0) / CODES)
    return (root * root * root).astype(BF)


def rank_of(owner):
    return (owner % 16) * 2 + owner // 16


def label_places(labels_ref, block, entry, chip):
    label = labels_ref[block : block + 1, entry * TOK : (entry + 1) * TOK].astype(jnp.int32)
    local = label - chip * 64
    inside = (label >= 0) & (local >= 0) & (local < 64)
    return jnp.where(inside, (local & 1) * 32 + (local >> 1), -1)


def block_rows(packed_ref, chip, core):
    parts = [packed_ref[chip, core, part * TOK : (part + 1) * TOK, :] for part in range(4)]
    return jnp.concatenate(parts, axis=1)


def tower_kernel(
    packed_ref, w_in_ref, w_out_ref, user_ref, rows_ref, labels_ref,
    key_scr, value_scr, query_scr, total_scr,
):
    parity = lax.axis_index("core")
    chip = lax.axis_index("z")

    shift = TOK - lax.rem(chip, 4) * 32
    row_at = lax.broadcasted_iota(jnp.int32, (16, TOK), 0)
    chip_row = lax.div(chip, 4)
    for block in range(CHIPS):
        extras = packed_ref[block, parity, WIDTH:PACK_ROWS, :].astype(F32)
        mine = pltpu.roll(extras, shift, 1)
        for slot in range(2):
            chosen = jnp.where(row_at == chip_row + 4 * slot, mine, 0.0)
            at = slot * CHIPS + block
            rows_ref[at : at + 1, :] = jnp.sum(chosen, axis=0, keepdims=True)
        labels_ref[block : block + 1, :] = jnp.concatenate(
            [extras[8 + entry : 9 + entry] for entry in range(4)], axis=1
        )

    def project(step, carry):
        pieces = [block_rows(packed_ref, 2 * step + n // 2, n % 2) for n in range(4)]
        rows = decode(jnp.concatenate(pieces, axis=0))
        at = pl.ds(pl.multiple_of(step * TILE, TILE), TILE)
        value_scr[at, :] = silu(dot(rows, w_in_ref[:, 512:1024])).astype(BF)
        key_scr[:, at] = silu(dot(w_in_ref[:, 1280:1536], rows, (((0,), (1,)), ((), ())))).astype(BF)
        return carry

    lax.fori_loop(0, 2 * HALF // TILE, project, 0)

    lane = lax.broadcasted_iota(jnp.int32, (TILE, 2 * DQK), 1)

    def tile(top, height, start, width, diagonal=None):
        if diagonal is not None:
            row = lax.broadcasted_iota(jnp.int32, (height, width), 0)
            key_at = lax.broadcasted_iota(jnp.int32, (height, width), 1) + diagonal[0]
            block = row // TOK + diagonal[1]
            allowed = key_at <= (2 * block + parity) * TOK + row % TOK
        weights = []
        for head in range(HEADS):
            keys = key_scr[(head // 2) * 2 * DQK : (head // 2 + 1) * 2 * DQK, pl.ds(start, width)]
            weight = half_silu(dot(query_scr[head, top : top + height], keys))
            if diagonal is not None:
                weight = jnp.where(allowed, weight, 0.0)
            weights.append(weight.astype(BF))
        for head in range(HEADS):
            values = value_scr[pl.ds(start, width), head * 128 : (head + 1) * 128]
            total_scr[top : top + height, head * 128 : (head + 1) * 128] += dot(weights[head], values)

    for group in range(HALF // TILE):
        rows = decode(
            jnp.concatenate([block_rows(packed_ref, 4 * group + n, parity) for n in range(4)], axis=0)
        )
        query = (silu(dot(rows, w_in_ref[:, 1024:1280])).astype(BF) * 0.0625).astype(BF)
        for head in range(HEADS):
            both = query[:, (head // 2) * 2 * DQK : (head // 2 + 1) * 2 * DQK]
            mine = (lane >= DQK) if head % 2 else (lane < DQK)
            query_scr[head] = jnp.where(mine, both, jnp.zeros_like(both))
        total_scr[...] = jnp.zeros_like(total_scr)
        base = group * 2 * TILE

        def earlier(step, carry):
            tile(0, TILE, pl.multiple_of(step * 2 * TILE, 2 * TILE), 2 * TILE)
            return carry

        lax.fori_loop(0, group, earlier, 0)
        for pair in range(2):
            top = pair * 2 * TOK
            first = base + 2 * top
            if pair:
                tile(top, 2 * TOK, base, TILE)
            tile(top, 2 * TOK, first, 2 * TOK, (0, 0))
            tile(top + TOK, TOK, first + 2 * TOK, 2 * TOK, (2 * TOK, 1))

        attended = total_scr[...]
        centered = attended - jnp.mean(attended, axis=-1, keepdims=True)
        variance = jnp.mean(centered * centered, axis=-1, keepdims=True)
        normed = centered * lax.rsqrt(variance + norm_eps)
        gate_units = silu(dot(rows, w_in_ref[:, 0:512]))
        mixed_rows = (normed * gate_units).astype(BF)
        updated = rows.astype(F32) + dot(mixed_rows, w_out_ref[...])
        scale = lax.rsqrt(jnp.sum(updated * updated, axis=-1, keepdims=True) + unit_eps)
        user_ref[group * TILE : (group + 1) * TILE, :] = (updated * scale).astype(BF)


def scores_kernel(
    table_ref, user_ref, rows_ref, labels_ref, exps_ref, hits_ref, exchange_ref, entry_scr
):
    chip = lax.axis_index("z")
    row_ids = lax.broadcasted_iota(jnp.int32, (32, TOK), 1).astype(F32)
    for owner in range(32):
        asked = jnp.broadcast_to(rows_ref[:, owner : owner + 1], (32, TOK))
        rows = dot((row_ids == asked).astype(BF), table_ref[rank_of(owner)])
        used = (asked >= 0.0).astype(F32)
        for slot in range(2):
            entry_scr[4, pl.ds(slot * 32 + owner, 16, stride=64), :] = used[
                slot * 16 : (slot + 1) * 16
            ]
            for part in range(4):
                entry_scr[part, pl.ds(slot * 32 + owner, 16, stride=64), :] = rows[
                    slot * 16 : (slot + 1) * 16, part * 128 : (part + 1) * 128
                ]
    slot_ids = lax.broadcasted_iota(jnp.int32, (64, TOK), 0)
    exchange_ref[...] = jnp.zeros_like(exchange_ref)
    for block in range(CHIPS):
        entries = jnp.concatenate(
            [entry_scr[part, block * 64 : (block + 1) * 64, :] for part in range(4)], axis=1
        ).astype(BF)
        scores = dot(entries, user_ref[block * TOK : (block + 1) * TOK, :], NT) * inverse_sharpness
        used = entry_scr[4, block * 64 : (block + 1) * 64, :] > 0.0
        exps = jnp.where(used, jnp.exp(scores), 0.0)
        exps_ref[block] = exps
        hits = jnp.zeros((64, TOK), F32)
        for entry in range(4):
            place = label_places(labels_ref, block, entry, chip)
            hits = hits + (slot_ids == place).astype(F32)
        hits_ref[block] = hits
        total = jnp.sum(exps, axis=0, keepdims=True)
        exchange_ref[:, block : block + 1, :] = jnp.broadcast_to(total[None], (CHIPS, 1, TOK))
        exchange_ref[block, 16:17, :] = jnp.sum(hits * scores, axis=0, keepdims=True)


def gradient_kernel(
    exps_ref, hits_ref, user_ref, exchange_ref, labels_ref, rows_ref,
    send_ref, loss_ref, grad_scr,
):
    chip = lax.axis_index("z")
    sums = jnp.sum(exchange_ref[...], axis=0)
    positives = jnp.zeros((CHIPS, TOK), F32)
    for entry in range(4):
        positives = positives + (labels_ref[:, entry * TOK : (entry + 1) * TOK] >= 0.0).astype(F32)
    divisor = jnp.maximum(positives, 1.0)
    totals = sums[0:16]
    own = lax.broadcasted_iota(jnp.int32, (CHIPS, TOK), 0) == chip
    losses = (positives * jnp.log(totals) - sums[16:17]) / divisor
    loss_ref[...] = jnp.sum(jnp.where(own, losses, 0.0), axis=0, keepdims=True)
    exp_scale = positives / (divisor * totals)
    hit_scale = 1.0 / divisor
    for block in range(CHIPS):
        score_grad = (
            exps_ref[block] * exp_scale[block : block + 1]
            - hits_ref[block] * hit_scale[block : block + 1]
        ).astype(BF)
        grads = dot(score_grad, user_ref[block * TOK : (block + 1) * TOK, :]) * inverse_sharpness
        for slot in range(2):
            for part in range(4):
                for side in range(2):
                    at = side * SEND_ROWS + part * 32 + slot * 16 + block
                    first = slot * 32 + side * 16
                    grad_scr[pl.ds(at, 16, stride=2 * SEND_ROWS), :] = grads[
                        first : first + 16, part * 128 : (part + 1) * 128
                    ]
    sender = lax.axis_index("item") * 2 + lax.axis_index("core")
    at = lax.broadcasted_iota(jnp.int32, (32, TOK), 0) + (sender & 3) * 32
    spread = (lax.broadcasted_iota(jnp.int32, (32, TOK), 1) == at).astype(BF)
    index = dot(rows_ref[...].astype(BF), spread, (((0,), (0,)), ((), ())))[0:32]
    zeros = jnp.zeros((16, TOK), F32)
    for side in range(2):
        for extra in range(SEND_ROWS - TOK):
            rows = zeros if extra else index[side * 16 : (side + 1) * 16]
            grad_scr[pl.ds(side * SEND_ROWS + TOK + extra, 16, stride=2 * SEND_ROWS), :] = rows
    send_ref[...] = grad_scr[...].astype(BF)


def owner_kernel(
    arrived_ref, index_ref, hidden_in_ref, raw_ref, w_in_ref, w_out_ref, gradient_ref, rows_scr
):
    row_ids = lax.broadcasted_iota(jnp.int32, (TOK, TOK), 0).astype(F32)
    row_grad = jnp.zeros((TOK, WIDTH), F32)
    for group in range(8):
        index = jnp.zeros((1, TOK), F32)
        for member in range(4):
            sender = group * 4 + member
            index = index + index_ref[sender : sender + 1, :]
            for part in range(4):
                rows_scr[member * 32 : (member + 1) * 32, part * 128 : (part + 1) * 128] = arrived_ref[
                    sender, part * 32 : (part + 1) * 32, :
                ]
        pick = (row_ids == index).astype(BF)
        row_grad = row_grad + dot(pick, rows_scr[...])
    raw = raw_ref[...]
    inv_norm = lax.rsqrt(jnp.sum(raw * raw, axis=-1, keepdims=True) + unit_eps)
    unit = raw * inv_norm
    raw_grad = (row_grad - unit * jnp.sum(unit * row_grad, axis=-1, keepdims=True)) * inv_norm
    hidden_grad = split_product(raw_grad, w_out_ref[...])
    hidden_in = hidden_in_ref[...]
    sigma = 0.5 * jnp.tanh(0.5 * hidden_in) + 0.5
    input_grad = hidden_grad * (sigma * (1.0 + hidden_in * (1.0 - sigma)))
    gradient_ref[...] = split_product(input_grad, w_in_ref[...])


def on_device(
    history, w_in, w_out, item_table, w_item_in, w_item_out, req_rows, req_counts, labels
):
    with jax.named_scope("prepare"):
        packed, hidden_in, raw_embed, copies = call(
            prepare_kernel,
            (
                jax.ShapeDtypeStruct((PACK_ROWS, 128), jnp.int16),
                jax.ShapeDtypeStruct((TOK, HIDDEN), F32),
                jax.ShapeDtypeStruct((TOK, WIDTH), F32),
                jax.ShapeDtypeStruct((32, TOK, WIDTH), BF),
            ),
            7,
            limit=LARGE_LIMIT,
        )(
            history[0], req_rows[0, 0].T, req_counts[0], labels[0].T,
            item_table, w_item_in, w_item_out,
        )

    with jax.named_scope("table_copies"):
        table = lax.all_to_all(copies, ("item", "core"), split_axis=0, concat_axis=0, tiled=True)

    with jax.named_scope("history_gather"):
        gathered = lax.all_gather(packed, ("z", "core"), axis=0, tiled=True)

    with jax.named_scope("tower"):
        user_rows, asked_rows, label_rows = call(
            tower_kernel,
            (
                jax.ShapeDtypeStruct((HALF, WIDTH), BF),
                jax.ShapeDtypeStruct((32, TOK), F32),
                jax.ShapeDtypeStruct((CHIPS, WIDTH), F32),
            ),
            3,
            [
                pltpu.VMEM((HEADS * DQK, 2 * HALF), BF),
                pltpu.VMEM((2 * HALF, WIDTH), BF),
                pltpu.VMEM((HEADS, TILE, 2 * DQK), BF),
                pltpu.VMEM((TILE, WIDTH), F32),
            ],
            limit=TOWER_LIMIT,
        )(gathered.reshape(CHIPS, 2, PACK_ROWS, 128), w_in, w_out)

    with jax.named_scope("scores"):
        exps, hits, exchange = call(
            scores_kernel,
            (
                jax.ShapeDtypeStruct((CHIPS, 64, TOK), F32),
                jax.ShapeDtypeStruct((CHIPS, 64, TOK), F32),
                jax.ShapeDtypeStruct((CHIPS, 24, TOK), F32),
            ),
            4,
            [pltpu.VMEM((5, 1024, 128), F32)],
        )(table, user_rows, asked_rows, label_rows)

    with jax.named_scope("totals_exchange"):
        exchange = lax.all_to_all(exchange, "z", split_axis=0, concat_axis=0, tiled=True)

    with jax.named_scope("gradient_rows"):
        send, loss = call(
            gradient_kernel,
            (
                jax.ShapeDtypeStruct((32 * SEND_ROWS, 128), BF),
                jax.ShapeDtypeStruct((1, TOK), F32),
            ),
            6,
            [pltpu.VMEM((32 * SEND_ROWS, 128), F32)],
        )(exps, hits, user_rows, exchange, label_rows, asked_rows)

    with jax.named_scope("gradient_send"):
        arrived = lax.all_to_all(
            send.reshape(32, SEND_ROWS, 128), ("item", "core"), split_axis=0, concat_axis=0, tiled=True
        )

    with jax.named_scope("owner"):
        gradient = call(
            owner_kernel,
            jax.ShapeDtypeStruct((TOK, WIDTH), F32),
            6,
            [pltpu.VMEM((TOK, WIDTH), BF)],
        )(arrived, arrived[:, TOK].astype(F32), hidden_in, raw_embed, w_item_in, w_item_out)
    return (loss, gradient)


def solution(mesh):
    split = Mesh(mesh.devices.reshape(CHIPS, 2, 16), ("z", "core", "item"))
    rows = ("z", "core")
    placed = (
        P("item", rows, None),
        P(),
        P(),
        P(("z", "core", "item"), None),
        P(),
        P(),
        P("item", rows, None, None),
        P("item", rows, None),
        P("item", rows, None),
    )
    return jax.shard_map(
        on_device,
        mesh=split,
        in_specs=placed,
        out_specs=(P("item", rows), P(("z", "core", "item"), None)),
        check_vma=False,
    )
```
